128 devices in a mesh: gx: 16 (over z, x_lo, core), gy: 8 (over y, x_hi).
Axes of the slice: x: 4 (x_hi: 2, x_lo: 2; x = x_hi * 2 + x_lo), y: 4, z: 4, core: 2. Of those that a mesh axis runs over, the one named last changes fastest.
Arguments:
- adjoint_forcing: float32 [16, 3072, 3072], P(None, 'gx', 'gy'), may hold values from -6 to 6
- courant_x: bfloat16 [16, 3072, 3072], P(None, 'gx', 'gy'), may hold values from -0.44921875 to 0.44921875
- courant_y: bfloat16 [16, 3072, 3072], P(None, 'gx', 'gy'), may hold values from -0.44921875 to 0.44921875
- vertical_mix: bfloat16 [16, 3072, 3072], P(None, 'gx', 'gy'), may hold values from 0.019897461 to 0.23925781
- tile_block: int32 [32768], replicated, may hold values from 0 to 147455, as said below
- injection_level: int32 [32768], P(('gx', 'gy')), may hold values from 0 to 15
- plume_profile: float32 [16, 16], replicated, may hold values from 0 to 1
- burn_weight: bfloat16 [32768, 6400], P(('gx', 'gy')), may hold values from 0.19921875 to 1
Outputs:
- adjoint_start: float32 [16, 3072, 3072], P(None, 'gx', 'gy')
- emission_gradient: bfloat16 [32768, 6400], P(('gx', 'gy'))
The draws below stay inside these ranges and needn't reach their ends.
Inputs may be any that keep to these rules, and one draw needn't show every extreme that they name: `tile_block`: the tiles of one device lie on the columns of exactly 64 different devices, exactly 4 of them on each of those.
All inputs are finite; a program needn't handle non-finite values.
Results may differ from the reference program's by a relative error of at most 0.001.
Values sent between devices are 32-bit elements; how exact they have to be, the bound alone decides.
A program may use at most 192 MiB of HBM per device.

```python
import jax
import jax.numpy as jnp
from jax import lax

LEV = 16
CX = 192
CY = 384
TILES_DEV = 256
ITERS = 4
TB = 8
SUB = 100
NX = 3072
NY = 3072
SOURCES = 64
CAP = 4
TILES = 32768
FIRE = 6400
N_GX = 16
N_GY = 8


def draw_tile_block(key, part):
    processor_total = N_GX * N_GY
    key_hot, key_noise, key_order, key_local = jax.random.split(jax.random.fold_in(key, 17), 4)
    priority_order = jax.random.permutation(key_hot, processor_total)
    burning_extra_weight = jnp.where(priority_order < max(processor_total // 8, 1), 4096, 0).astype(jnp.int32)
    random_perturbation = jax.random.randint(key_noise, (processor_total, processor_total), 0, 1024)
    tile_priority_values = (random_perturbation + burning_extra_weight[None, :]) * processor_total + jnp.arange(processor_total, dtype=jnp.int32)[None, :]
    chosen = lax.top_k(tile_priority_values, SOURCES)[1].astype(jnp.int32)
    repeated = jnp.repeat(chosen, CAP, axis=1)
    shuffle = jax.random.randint(key_order, (processor_total, TILES_DEV), 0, 4096) * TILES_DEV + jnp.arange(TILES_DEV, dtype=jnp.int32)[None, :]
    slot_order = jnp.argsort(shuffle, axis=1)
    source = jnp.take_along_axis(repeated, slot_order, axis=1)
    per_x = CX // TB
    per_y = CY // TB
    local_block = jax.random.randint(key_local, (processor_total, TILES_DEV), 0, per_x * per_y)
    block_row = source // N_GY * per_x + local_block // per_y
    block_col = source % N_GY * per_y + local_block % per_y
    return (block_row * (NY // TB) + block_col).reshape(-1).astype(jnp.int32)


def place_ends(array, key, low, largest):
    longest = array.shape.index(max(array.shape))
    spots = []
    for shift in (0, 1):
        where = [jax.random.randint(jax.random.fold_in(key, axis), (), 0, length) for axis, length in enumerate(array.shape)]
        where[longest] = (where[longest] + shift) % array.shape[longest]
        spots.append(tuple(where))
    return array.at[spots[0]].set(low).at[spots[1]].set(largest)


def level_of(stream_key, shape, cuts, low, high):
    level, own = 1.0, jax.random.fold_in(stream_key, 6)
    for axis_at, parts in cuts:
        steps = jnp.exp(jax.random.uniform(jax.random.fold_in(own, axis_at), (parts,), jnp.float32, low / len(cuts), high / len(cuts)))
        level = level * jnp.repeat(steps, shape[axis_at] // parts).reshape([-1 if axis == axis_at else 1 for axis in range(len(shape))])
    return level


def gaussian(rng, dims, spread, reach, cuts=(), kind=jnp.bfloat16):
    level = level_of(rng, dims, cuts, -0.22, 0.18) if cuts else 1.0
    values = jax.random.normal(rng, dims, jnp.float32) * spread * level
    return jnp.minimum(jnp.maximum(values, -reach), reach).astype(kind)


def setup_inputs(seed: int = 0) -> dict:
    key_list = jax.random.split(jax.random.key(seed), 9)
    return {
        "adjoint_forcing": gaussian(key_list[0], (LEV, NX, NY), 1.0, 6.0, ((1, 16), (2, 8)), jnp.float32),
        "courant_x": jnp.clip(jax.random.uniform(key_list[1], (LEV, NX, NY), jnp.float32, -0.44921875, 0.44921875) * level_of(key_list[1], (LEV, NX, NY), ((1, 16), (2, 8)), -0.4, 0.0), -0.44921875, 0.44921875).astype(jnp.bfloat16),
        "courant_y": jnp.clip(jax.random.uniform(key_list[2], (LEV, NX, NY), jnp.float32, -0.44921875, 0.44921875) * level_of(key_list[2], (LEV, NX, NY), ((1, 16), (2, 8)), -0.4, 0.0), -0.44921875, 0.44921875).astype(jnp.bfloat16),
        "vertical_mix": jnp.clip(0.019897461 + 0.21936035 * jax.random.uniform(key_list[3], (LEV, NX, NY), jnp.float32) ** level_of(key_list[3], (LEV, NX, NY), ((1, 16), (2, 8)), -0.2, 0.2), 0.019897461, 0.23925781).astype(jnp.bfloat16),
        "tile_block": draw_tile_block(jax.random.fold_in(key_list[8], 71), 0),
        "injection_level": place_ends(jax.random.randint(key_list[5], (TILES,), 0, LEV), jax.random.fold_in(key_list[5], 1), 0, LEV - 1).astype(jnp.int32),
        "plume_profile": jnp.clip(jax.random.uniform(key_list[6], (LEV, LEV), jnp.float32, 0.0, 1.0), 0.0, 1.0),
        "burn_weight": jnp.clip(0.19921875 + 0.80078125 * jax.random.uniform(key_list[7], (TILES, FIRE), jnp.float32) ** level_of(key_list[7], (TILES, FIRE), ((0, 128),), -0.2, 0.2), 0.19921875, 1.0).astype(jnp.bfloat16),
    }


def diffuse(state_field, mixing):
    flux = mixing[:-1] * (state_field[1:] - state_field[:-1])
    zero_layer = jnp.zeros_like(state_field[:1])
    upper = jnp.concatenate([flux, zero_layer], 0)
    lower = jnp.concatenate([zero_layer, flux], 0)
    return state_field + upper - lower


def advect(padded, speed_x, speed_y):
    center = padded[:, 1:-1, 1:-1]
    keep = 1.0 - jnp.abs(speed_x) - jnp.abs(speed_y)
    total = keep * center
    total = total + jnp.maximum(speed_x, 0.0) * padded[:, 2:, 1:-1]
    total = total + jnp.maximum(-speed_x, 0.0) * padded[:, :-2, 1:-1]
    total = total + jnp.maximum(speed_y, 0.0) * padded[:, 1:-1, 2:]
    total = total + jnp.maximum(-speed_y, 0.0) * padded[:, 1:-1, :-2]
    return total


def reference(adjoint_forcing, courant_x, courant_y, vertical_mix, tile_block, injection_level, plume_profile, burn_weight):
    speed_x = courant_x.astype(jnp.float32)
    speed_y = courant_y.astype(jnp.float32)
    mixing = vertical_mix.astype(jnp.float32)
    state_field = adjoint_forcing
    for repeat_index in range(ITERS):
        blended_concentration = diffuse(state_field, mixing)
        padded = jnp.pad(blended_concentration, ((0, 0), (1, 1), (1, 1)))
        state_field = advect(padded, speed_x, speed_y)
    blocks_y = NY // TB
    row_starts = ((tile_block // blocks_y) * TB).astype(jnp.int32)
    col_starts = ((tile_block % blocks_y) * TB).astype(jnp.int32)

    def cut_block(start_row, start_col):
        piece = lax.dynamic_slice(state_field, (jnp.int32(0), start_row, start_col), (LEV, TB, TB))
        return piece.reshape(LEV, TB * TB)

    pieces = jax.vmap(cut_block)(row_starts, col_starts)
    onehot = (injection_level[:, None] == jnp.arange(LEV, dtype=jnp.int32)[None, :]).astype(jnp.float32)
    weights = jnp.dot(onehot, plume_profile, precision=lax.Precision.HIGHEST)
    column = jnp.einsum("kl,klc->kc", weights, pieces, precision=lax.Precision.HIGHEST)
    tiles_total = tile_block.shape[0]
    gradient = burn_weight.astype(jnp.float32).reshape(tiles_total, TB * TB, SUB) * column[:, :, None]
    return state_field, gradient.reshape(tiles_total, TB * TB * SUB).astype(jnp.bfloat16)
```

```python
import functools

import jax
import jax.numpy as jnp
from jax import lax
from jax.experimental import pallas as pl
from jax.experimental.pallas import tpu as pltpu
from jax.sharding import PartitionSpec as P

ITERS = 4
TB = 8
SUB = 100
MESH = pl.DeviceIdType.MESH
MIB = 1024 * 1024


def fori(low, high, body):
    def step(i, carry):
        body(i)
        return carry

    lax.fori_loop(low, high, step, 0)


def stencil_kernel(
    f_hbm, cu_hbm, cv_hbm, k_hbm, out,
    field, cu, cv, mix, work, ysend, yrecv,
    load_sem, save_sem, xs_sem, xr_sem, ys_sem, yr_sem,
):
    levels, rows, cols = field.shape
    tiles = cols // 128
    groups = rows // 16
    inner = (groups - 2) // 2
    gx, gy = lax.axis_index("gx"), lax.axis_index("gy")
    nx, ny = lax.axis_size("gx"), lax.axis_size("gy")
    have_x = (gx > 0, gx < nx - 1)
    have_y = (gy > 0, gy < ny - 1)
    peer_x = ((jnp.maximum(gx - 1, 0), gy), (jnp.minimum(gx + 1, nx - 1), gy))
    peer_y = ((gx, jnp.maximum(gy - 1, 0)), (gx, jnp.minimum(gy + 1, ny - 1)))
    lane = lax.broadcasted_iota(jnp.int32, (16, 128), 1)

    pieces = ((0, 16), (rows - 16, 16), (16, 16 * inner), (16 + 16 * inner, 16 * inner))
    loads = []
    for a, (src, dst) in enumerate(((f_hbm, field), (k_hbm, mix))):
        loads.append([
            pltpu.make_async_copy(
                src.at[:, pl.ds(at, size), :], dst.at[:, pl.ds(at, size), :], load_sem.at[a, p]
            )
            for p, (at, size) in enumerate(pieces)
        ])
    saves = [
        pltpu.make_async_copy(
            field.at[:, pl.ds(at, size), :], out.at[:, pl.ds(at, size), :], save_sem.at[p]
        )
        for p, (at, size) in enumerate(pieces)
    ]
    late = [
        pltpu.make_async_copy(cu_hbm, cu, load_sem.at[2, 0]),
        pltpu.make_async_copy(cv_hbm, cv, load_sem.at[2, 1]),
    ]
    for p in range(4):
        loads[0][p].start()
        loads[1][p].start()
    for copy in late:
        copy.start()

    zero_row = jnp.zeros((1, 128), jnp.float32)

    def clear(l):
        for b in range(2):
            for j in range(tiles):
                work[b, l, j, 7:8, :] = zero_row
                work[b, l, j, rows + 8 : rows + 9, :] = zero_row

    fori(0, levels, clear)
    yrecv[...] = jnp.zeros_like(yrecv)

    barrier = pltpu.get_barrier_semaphore()
    for have, peers in ((have_x, peer_x), (have_y, peer_y)):
        for side in range(2):
            @pl.when(have[side])
            def _():
                pl.semaphore_signal(barrier, inc=1, device_id=peers[side], device_id_type=MESH)
    expected = sum(h.astype(jnp.int32) for h in have_x + have_y)
    pl.semaphore_wait(barrier, expected)

    def x_copy(n, side):
        b = lax.rem(n, 2)
        src, dst = ((8, rows + 8), (rows + 7, 7))[side]
        return pltpu.make_async_remote_copy(
            src_ref=work.at[b, :, :, pl.ds(src, 1), :],
            dst_ref=work.at[b, :, :, pl.ds(dst, 1), :],
            send_sem=xs_sem.at[n, side],
            recv_sem=xr_sem.at[n, side],
            device_id=peer_x[side],
            device_id_type=MESH,
        )

    def y_copy(n, side, chunk):
        return pltpu.make_async_remote_copy(
            src_ref=ysend.at[n, side, chunk],
            dst_ref=yrecv.at[n, side, chunk],
            send_sem=ys_sem.at[n, side, chunk],
            recv_sem=yr_sem.at[n, side, chunk],
            device_id=peer_y[side],
            device_id_type=MESH,
        )

    def send_x(n):
        for side in range(2):
            @pl.when(have_x[side])
            def _():
                x_copy(n, side).start()

    def send_y(n, chunk):
        for side in range(2):
            @pl.when(have_y[side])
            def _():
                y_copy(n, side, chunk).start()

    def await_x(n):
        for side in range(2):
            @pl.when(have_x[side])
            def _():
                x_copy(n, 1 - side).wait_recv()

    def await_y(n, chunk):
        for side in range(2):
            @pl.when(have_y[side])
            def _():
                y_copy(n, 1 - side, chunk).wait_recv()

    def await_x_sent(n):
        for side in range(2):
            @pl.when(have_x[side])
            def _():
                x_copy(n, side).wait_send()

    def mixed(values, i, j):
        at = pl.multiple_of(16 * i, 16)
        result, before = [], None
        for l in range(levels):
            total = values[l]
            if l < levels - 1:
                k = mix[l, pl.ds(at, 16), 128 * j : 128 * j + 128].astype(jnp.float32)
                flux = k * (values[l + 1] - values[l])
                total = total + flux
            if before is not None:
                total = total - before
            before = flux
            result.append(total)
        return result

    def store_mixed(n, values, i, j, m, chunk):
        b = lax.rem(n, 2)
        at = pl.multiple_of(8 + 16 * i, 8)
        result = mixed(values, i, j)
        for l in range(levels):
            work[b, l, j, pl.ds(at, 16), :] = result[l]
        for side, tile, own in ((0, 0, 0), (1, tiles - 1, 127)):
            if j == tile:
                packed = result[0] if own == 0 else pltpu.roll(result[0], 1, 1)
                for l in range(1, levels):
                    moved = pltpu.roll(result[l], (l - own) % 128, 1)
                    packed = jnp.where(lane == l, moved, packed)
                packed = pltpu.roll(packed, 16 * m, 1)
                old = ysend[n, side, chunk]
                ysend[n, side, chunk] = jnp.where(lane // 16 == m, packed, old)

    def moved_by_wind(n, i, j, m, chunk):
        b = lax.rem(n + 1, 2)
        at = pl.multiple_of(16 * i, 16)
        here = 8 + 16 * i
        before = after = None
        if j == 0:
            before = pltpu.roll(yrecv[n - 1, 1, chunk], lax.rem(128 - 16 * m, 128), 1)
        if j == tiles - 1:
            after = pltpu.roll(yrecv[n - 1, 0, chunk], lax.rem(128 - 16 * m, 128), 1)
        values = []
        for l in range(levels):
            c = work[b, l, j, pl.ds(here, 16), :]
            up = work[b, l, j, pl.ds(here + 1, 16), :]
            down = work[b, l, j, pl.ds(here - 1, 16), :]
            if j == 0:
                left = pltpu.roll(before, 127 - l, 1)
            else:
                left = work[b, l, j - 1, pl.ds(here, 16), :]
            if j == tiles - 1:
                right = pltpu.roll(after, (128 - l) % 128, 1) if l else after
            else:
                right = work[b, l, j + 1, pl.ds(here, 16), :]
            left = pltpu.roll(jnp.where(lane == 127, left, c), 1, 1)
            right = pltpu.roll(jnp.where(lane == 0, right, c), 127, 1)
            su = cu[l, pl.ds(at, 16), 128 * j : 128 * j + 128].astype(jnp.float32)
            sv = cv[l, pl.ds(at, 16), 128 * j : 128 * j + 128].astype(jnp.float32)
            total = c + jnp.abs(su) * (jnp.where(su > 0, up, down) - c)
            total = total + jnp.abs(sv) * (jnp.where(sv > 0, right, left) - c)
            values.append(total)
        return values

    def run(n, mode):
        def group(i, m, chunk):
            at = pl.multiple_of(16 * i, 16)
            for j in range(tiles):
                if mode == "first":
                    values = [
                        field[l, pl.ds(at, 16), 128 * j : 128 * j + 128] for l in range(levels)
                    ]
                else:
                    values = moved_by_wind(n, i, j, m, chunk)
                if mode == "last":
                    for l in range(levels):
                        field[l, pl.ds(at, 16), 128 * j : 128 * j + 128] = values[l]
                else:
                    store_mixed(n, values, i, j, m, chunk)

        if mode == "first":
            for p in range(2):
                loads[0][p].wait()
                loads[1][p].wait()
        else:
            await_x(n - 1)
            await_y(n - 1, 0)
            if mode == "middle":
                @pl.when(n >= 2)
                def _():
                    await_x_sent(n - 2)
        fori(0, 2, lambda m: group(m * (groups - 1), m, 0))
        if mode == "last":
            saves[0].start()
            saves[1].start()
        else:
            send_x(n)
            send_y(n, 0)

        def chunk_of(c):
            if mode != "first":
                await_y(n - 1, c + 1)
            fori(0, inner, lambda m: group(1 + c * inner + m, m, c + 1))
            if mode != "last":
                send_y(n, c + 1)

        if mode == "first":
            for c in range(2):
                loads[0][2 + c].wait()
                loads[1][2 + c].wait()
                chunk_of(c)
        elif mode == "last":
            for c in range(2):
                chunk_of(c)
                saves[2 + c].start()
        else:
            fori(0, 2, chunk_of)

    run(0, "first")
    for copy in late:
        copy.wait()
    fori(1, ITERS, lambda n: run(n, "middle"))
    run(ITERS, "last")
    for save in saves:
        save.wait()
    for n in (ITERS - 2, ITERS - 1):
        await_x_sent(n)
    for n in range(ITERS):
        for side in range(2):
            @pl.when(have_y[side])
            def _():
                for chunk in range(3):
                    y_copy(n, side, chunk).wait_send()


def stencil(f, cu, cv, k):
    levels, rows, cols = f.shape
    any_space = pl.BlockSpec(memory_space=pl.ANY)
    tiles = cols // 128
    return pl.pallas_call(
        stencil_kernel,
        out_shape=jax.ShapeDtypeStruct(f.shape, jnp.float32),
        in_specs=[any_space] * 4,
        out_specs=any_space,
        scratch_shapes=[
            pltpu.VMEM(f.shape, jnp.float32),
            pltpu.VMEM(f.shape, jnp.bfloat16),
            pltpu.VMEM(f.shape, jnp.bfloat16),
            pltpu.VMEM(f.shape, jnp.bfloat16),
            pltpu.VMEM((2, levels, tiles, rows + 16, 128), jnp.float32),
            pltpu.VMEM((ITERS, 2, 3, 16, 128), jnp.float32),
            pltpu.VMEM((ITERS, 2, 3, 16, 128), jnp.float32),
            pltpu.SemaphoreType.DMA((3, 4)),
            pltpu.SemaphoreType.DMA((4,)),
            pltpu.SemaphoreType.DMA((ITERS, 2)),
            pltpu.SemaphoreType.DMA((ITERS, 2)),
            pltpu.SemaphoreType.DMA((ITERS, 2, 3)),
            pltpu.SemaphoreType.DMA((ITERS, 2, 3)),
        ],
        compiler_params=pltpu.CompilerParams(
            collective_id=0, has_side_effects=True, vmem_limit_bytes=58 * MIB
        ),
        name="stencil",
    )(f, cu, cv, k)


def gather_kernel(table, profile, field, out):
    levels = field.shape[0]
    ny, nx = out.shape[0], out.shape[1]
    lane = lax.broadcasted_iota(jnp.int32, (8, 128), 1)
    sub = lax.broadcasted_iota(jnp.int32, (8, 128), 0)
    mine = lane // 8 % 8 == sub

    def device(d):
        g, p = d // ny, lax.rem(d, ny)
        for pair in range(2):
            found = []
            for h in range(2):
                q = 4 * (4 * d + 2 * pair + h)
                row = pl.multiple_of(table[q], 8)
                col = pl.multiple_of(table[q + 1], 128)
                shift = table[q + 2]
                weight = table[q + 3]
                acc = None
                for l in range(levels):
                    term = profile[weight + l] * field[l, pl.ds(row, 8), pl.ds(col, 128)]
                    acc = term if acc is None else acc + term
                found.append(pltpu.roll(acc, shift, 1))
            both = jnp.where(lane < 64, found[0], found[1])
            for bit in (1, 2, 4):
                both = jnp.where(sub // bit % 2 == 1, pltpu.roll(both, 8 * bit, 1), both)
            both = jnp.where(mine, both, 0.0)
            out[p, g, pair : pair + 1, :] = jnp.sum(both, axis=0, keepdims=True)

    fori(0, nx * ny, device)


def gather(table, profile, field, nx, ny):
    smem = pl.BlockSpec(memory_space=pltpu.SMEM)
    vmem = pl.BlockSpec(memory_space=pltpu.VMEM)
    return pl.pallas_call(
        gather_kernel,
        out_shape=jax.ShapeDtypeStruct((ny, nx, 2, 128), jnp.float32),
        in_specs=[smem, smem, vmem],
        out_specs=vmem,
        compiler_params=pltpu.CompilerParams(vmem_limit_bytes=24 * MIB),
        name="gather",
    )(table, profile, field)


def exchange_kernel(rows, out, held, send1, recv1, send2, recv2):
    ny, nx = rows.shape[0], rows.shape[1]
    gx, gy = lax.axis_index("gx"), lax.axis_index("gy")
    barrier = pltpu.get_barrier_semaphore()

    def greet_y(o):
        pl.semaphore_signal(
            barrier, inc=1, device_id=(gx, lax.rem(gy + o, ny)), device_id_type=MESH
        )

    def greet_x(o):
        pl.semaphore_signal(
            barrier, inc=1, device_id=(lax.rem(gx + o, nx), gy), device_id_type=MESH
        )

    fori(1, ny, greet_y)
    fori(1, nx, greet_x)
    pl.semaphore_wait(barrier, nx + ny - 2)

    def first(o):
        to = lax.rem(gy + o, ny)
        return pltpu.make_async_remote_copy(
            src_ref=rows.at[to],
            dst_ref=held.at[gy],
            send_sem=send1.at[o],
            recv_sem=recv1.at[o],
            device_id=(gx, to),
            device_id_type=MESH,
        )

    def second(o):
        to = lax.rem(gx + o, nx)
        return pltpu.make_async_remote_copy(
            src_ref=held.at[:, to],
            dst_ref=out.at[gx],
            send_sem=send2.at[o],
            recv_sem=recv2.at[o],
            device_id=(to, gy),
            device_id_type=MESH,
        )

    fori(1, ny, lambda o: first(o).start())
    held[gy] = rows[gy]
    fori(1, ny, lambda o: first(o).wait_recv())
    fori(1, nx, lambda o: second(o).start())
    out[gx] = held[:, gx]
    fori(1, nx, lambda o: second(o).wait_recv())
    fori(1, ny, lambda o: first(o).wait_send())
    fori(1, nx, lambda o: second(o).wait_send())


def exchange(rows):
    ny, nx = rows.shape[0], rows.shape[1]
    vmem = pl.BlockSpec(memory_space=pltpu.VMEM)
    return pl.pallas_call(
        exchange_kernel,
        out_shape=jax.ShapeDtypeStruct((nx, ny, 2, 128), jnp.float32),
        in_specs=[vmem],
        out_specs=vmem,
        scratch_shapes=[
            pltpu.VMEM(rows.shape, jnp.float32),
            pltpu.SemaphoreType.DMA((ny,)),
            pltpu.SemaphoreType.DMA((ny,)),
            pltpu.SemaphoreType.DMA((nx,)),
            pltpu.SemaphoreType.DMA((nx,)),
        ],
        compiler_params=pltpu.CompilerParams(
            collective_id=1, has_side_effects=True, vmem_limit_bytes=16 * MIB
        ),
        name="exchange",
    )(rows)


def gradient_kernel(rows, where, burn, out, column):
    step = pl.program_id(0)
    tiles_dev, width = burn.shape

    @pl.when(step == 0)
    def _():
        values = rows[...]
        high = values.astype(jnp.bfloat16)
        rest = values - high.astype(jnp.float32)
        mid = rest.astype(jnp.bfloat16)
        low = (rest - mid.astype(jnp.float32)).astype(jnp.bfloat16)
        index = where[:, 0:1]
        half = where[:, 1:2]
        count = values.shape[0]
        onehot = (lax.broadcasted_iota(jnp.int32, (tiles_dev, count), 1) == index).astype(
            jnp.float32
        ).astype(jnp.bfloat16)
        lane = lax.broadcasted_iota(jnp.int32, (tiles_dev, 128), 1)
        parts = []
        for part in (high, mid, low):
            picked = jnp.dot(onehot, part, preferred_element_type=jnp.float32)
            parts.append(jnp.where(half == 1, pltpu.roll(picked, 64, 1), picked))
        column[:, 0:128] = jnp.where(lane < 64, parts[0], pltpu.roll(parts[1], 64, 1)).astype(
            jnp.bfloat16
        )
        column[:, 128:256] = jnp.where(lane < 64, parts[2], 0.0).astype(jnp.bfloat16)

    cell = step * width + lax.broadcasted_iota(jnp.int32, (64, width), 1)
    start = SUB * lax.broadcasted_iota(jnp.int32, (64, width), 0)
    spread = ((cell >= start) & (cell < start + SUB)).astype(jnp.float32).astype(jnp.bfloat16)
    spread = jnp.concatenate([spread] * 4, axis=0)
    expanded = jnp.dot(column[...], spread, preferred_element_type=jnp.float32)
    out[...] = (burn[...].astype(jnp.float32) * expanded).astype(jnp.bfloat16)


def gradient(rows, where, burn):
    tiles_dev, fire = burn.shape
    width = 1280
    return pl.pallas_call(
        gradient_kernel,
        grid=(fire // width,),
        out_shape=jax.ShapeDtypeStruct(burn.shape, jnp.bfloat16),
        in_specs=[
            pl.BlockSpec(rows.shape, lambda s: (0, 0)),
            pl.BlockSpec(where.shape, lambda s: (0, 0)),
            pl.BlockSpec((tiles_dev, width), lambda s: (0, s)),
        ],
        out_specs=pl.BlockSpec((tiles_dev, width), lambda s: (0, s)),
        scratch_shapes=[pltpu.VMEM((tiles_dev, 256), jnp.bfloat16)],
        compiler_params=pltpu.CompilerParams(vmem_limit_bytes=24 * MIB),
        name="gradient",
    )(rows, where, burn)


def locate(block_ids, per_x, per_y, blocks_y, gy_count):
    block_row = block_ids // blocks_y
    block_col = block_ids % blocks_y
    source = block_row // per_x * gy_count + block_col // per_y
    local_block = block_row % per_x * per_y + block_col % per_y
    return (source, local_block)


def on_device(
    adjoint_forcing,
    courant_x,
    courant_y,
    vertical_mix,
    tile_block,
    injection_level,
    plume_profile,
    burn_weight,
):
    levels, width_x, width_y = adjoint_forcing.shape
    gx_count = lax.axis_size("gx")
    gy_count = lax.axis_size("gy")
    total = gx_count * gy_count
    tiles_dev = injection_level.shape[0]
    capacity = 4
    per_x = width_x // TB
    per_y = width_y // TB
    blocks_y = per_y * gy_count
    me = lax.axis_index(("gx", "gy"))
    all_levels = lax.all_gather(injection_level, ("gx", "gy"), tiled=True).reshape(total, tiles_dev)
    slot_table = tile_block.reshape(total, tiles_dev)
    source, local_block = locate(slot_table, per_x, per_y, blocks_y, gy_count)
    is_mine = (source == me).astype(jnp.int32)
    upto = jnp.triu(jnp.ones((tiles_dev, tiles_dev), jnp.bfloat16))
    rank = jnp.dot(
        is_mine.astype(jnp.bfloat16), upto, preferred_element_type=jnp.float32
    ).astype(jnp.int32) - 1
    slots = jnp.arange(capacity, dtype=jnp.int32)
    hits = (is_mine[:, None, :] == 1) & (rank[:, None, :] == slots[None, :, None])
    local = jnp.sum(jnp.where(hits, local_block[:, None, :], 0), axis=2)
    level = jnp.sum(jnp.where(hits, all_levels[:, None, :], 0), axis=2)
    block_row = local // per_y
    lane_at = local % per_y * TB
    shift = (64 * (slots % 2)[None, :] - lane_at) % 128
    table = jnp.stack(
        [block_row * TB, lane_at // 128 * 128, shift, level * levels], axis=2
    ).reshape(-1)

    state_field = stencil(adjoint_forcing, courant_x, courant_y, vertical_mix)
    rows = gather(table, plume_profile.reshape(-1), state_field, gx_count, gy_count)
    rows = exchange(rows).reshape(total * 2, 128)

    own = lax.dynamic_slice_in_dim(source, me, 1, 0).reshape(tiles_dev)
    positions = jnp.arange(tiles_dev, dtype=jnp.int32)
    earlier = (own[None, :] == own[:, None]) & (positions[None, :] <= positions[:, None])
    arrival = jnp.sum(earlier.astype(jnp.int32), axis=1) - 1
    where = jnp.stack([own * 2 + arrival // 2, arrival % 2], axis=1)
    return (state_field, gradient(rows, where, burn_weight))


def solution(mesh):
    return jax.shard_map(
        on_device,
        mesh=mesh,
        in_specs=(
            P(None, "gx", "gy"),
            P(None, "gx", "gy"),
            P(None, "gx", "gy"),
            P(None, "gx", "gy"),
            P(),
            P(("gx", "gy")),
            P(),
            P(("gx", "gy"), None),
        ),
        out_specs=(P(None, "gx", "gy"), P(("gx", "gy"), None)),
        check_vma=False,
    )
```

```python
import functools

import jax
import jax.numpy as jnp
from jax import lax
from jax.experimental import pallas as pl
from jax.experimental.pallas import tpu as pltpu
from jax.sharding import PartitionSpec as P

ITERS = 4
TB = 8
SUB = 100
MESH = pl.DeviceIdType.MESH
MIB = 1024 * 1024


def fori(low, high, body):
    def step(i, carry):
        body(i)
        return carry

    lax.fori_loop(low, high, step, 0)


def stencil_kernel(
    f_hbm, cu_hbm, cv_hbm, k_hbm, own, out, shared,
    field, cu, cv, mix, work, ysend, yrecv, held,
    load_sem, save_sem, xs_sem, xr_sem, ys_sem, yr_sem,
    send1, recv1, send2, recv2,
):
    levels, rows, cols = field.shape
    tiles = cols // 128
    groups = rows // 16
    chunks = groups // 2
    early = max(1, (chunks - 1) // 2)
    gx, gy = lax.axis_index("gx"), lax.axis_index("gy")
    nx, ny = lax.axis_size("gx"), lax.axis_size("gy")
    have_x = (gx > 0, gx < nx - 1)
    have_y = (gy > 0, gy < ny - 1)
    peer_x = ((jnp.maximum(gx - 1, 0), gy), (jnp.minimum(gx + 1, nx - 1), gy))
    peer_y = ((gx, jnp.maximum(gy - 1, 0)), (gx, jnp.minimum(gy + 1, ny - 1)))
    lane = lax.broadcasted_iota(jnp.int32, (16, 128), 1)
    odd = lane % 2 == 1

    pieces = [(0, 16, 0), (rows - 16, 16, 0), (16, 32 * early, 1)]
    if chunks - 1 > early:
        pieces.append((16 + 32 * early, 32 * (chunks - 1 - early), 1 + early))
    bounds = sorted({first for _, _, first in pieces}) + [chunks]

    def parts_copy(src, dst, sem):
        return [
            pltpu.make_async_copy(
                src.at[:, pl.ds(at, size), :], dst.at[:, pl.ds(at, size), :], sem.at[p]
            )
            for p, (at, size, _) in enumerate(pieces)
        ]

    load_f = parts_copy(f_hbm, field, load_sem.at[0])
    load_k = parts_copy(k_hbm, mix, load_sem.at[1])
    saves = parts_copy(field, out, save_sem)
    late = [
        pltpu.make_async_copy(cu_hbm, cu, load_sem.at[2, 0]),
        pltpu.make_async_copy(cv_hbm, cv, load_sem.at[2, 1]),
    ]
    for p in range(len(pieces)):
        load_f[p].start()
        load_k[p].start()
    for copy in late:
        copy.start()

    zero_row = jnp.zeros((1, 128), jnp.float32)

    def clear(l):
        for b in range(2):
            for j in range(tiles):
                work[b, l, j, 7:8, :] = zero_row
                work[b, l, j, rows + 8 : rows + 9, :] = zero_row

    fori(0, levels, clear)
    yrecv[...] = jnp.zeros_like(yrecv)

    barrier = pltpu.get_barrier_semaphore()

    def greet_y(o):
        pl.semaphore_signal(
            barrier, inc=1, device_id=(gx, lax.rem(gy + o, ny)), device_id_type=MESH
        )

    def greet_x(o):
        pl.semaphore_signal(
            barrier, inc=1, device_id=(lax.rem(gx + o, nx), gy), device_id_type=MESH
        )

    fori(1, ny, greet_y)
    fori(1, nx, greet_x)
    pl.semaphore_wait(barrier, nx + ny - 2)

    def share_y(o):
        return pltpu.make_async_remote_copy(
            src_ref=own,
            dst_ref=held.at[gy],
            send_sem=send1.at[o],
            recv_sem=recv1.at[o],
            device_id=(gx, lax.rem(gy + o, ny)),
            device_id_type=MESH,
        )

    def share_x(o):
        return pltpu.make_async_remote_copy(
            src_ref=held,
            dst_ref=shared.at[gx],
            send_sem=send2.at[o],
            recv_sem=recv2.at[o],
            device_id=(lax.rem(gx + o, nx), gy),
            device_id_type=MESH,
        )

    fori(1, ny, lambda o: share_y(o).start())
    held[gy] = own[...]

    def x_copy(n, side):
        b = lax.rem(n, 2)
        src, dst = ((8, rows + 8), (rows + 7, 7))[side]
        return pltpu.make_async_remote_copy(
            src_ref=work.at[b, :, :, pl.ds(src, 1), :],
            dst_ref=work.at[b, :, :, pl.ds(dst, 1), :],
            send_sem=xs_sem.at[n, side],
            recv_sem=xr_sem.at[n, side],
            device_id=peer_x[side],
            device_id_type=MESH,
        )

    def y_copy(n, side, chunk):
        return pltpu.make_async_remote_copy(
            src_ref=ysend.at[n, chunk],
            dst_ref=yrecv.at[n, side, chunk],
            send_sem=ys_sem.at[n, side, chunk],
            recv_sem=yr_sem.at[n, side, chunk],
            device_id=peer_y[side],
            device_id_type=MESH,
        )

    def send_x(n):
        for side in range(2):
            @pl.when(have_x[side])
            def _():
                x_copy(n, side).start()

    def send_y(n, chunk):
        for side in range(2):
            @pl.when(have_y[side])
            def _():
                y_copy(n, side, chunk).start()

    def await_x(n):
        for side in range(2):
            @pl.when(have_x[side])
            def _():
                x_copy(n, 1 - side).wait_recv()

    def await_y(n, chunk):
        for side in range(2):
            @pl.when(have_y[side])
            def _():
                y_copy(n, 1 - side, chunk).wait_recv()

    def await_x_sent(n):
        for side in range(2):
            @pl.when(have_x[side])
            def _():
                x_copy(n, side).wait_send()

    def mixed(values, at, j):
        result, before = [], None
        for l in range(levels):
            total = values[l]
            if l < levels - 1:
                k = mix[l, pl.ds(at, 16), 128 * j : 128 * j + 128].astype(jnp.float32)
                flux = k * (values[l + 1] - values[l])
                total = total + flux
            if before is not None:
                total = total - before
            before = flux
            result.append(total)
        return result

    def pack(first, last, m):
        packed = None
        for l in range(levels):
            ends = jnp.where(lane == 0, first[l], last[l])
            if l:
                moved = pltpu.roll(ends, 2 * l, 1)
                packed = jnp.where((lane == 2 * l) | (lane == 2 * l - 1), moved, packed)
            else:
                packed = ends
        return packed if m == 0 else pltpu.roll(packed, 32 * m, 1)

    def moved_by_wind(b, at, here, j, halo):
        values = []
        for l in range(levels):
            c = work[b, l, j, pl.ds(here, 16), :]
            up = work[b, l, j, pl.ds(here + 1, 16), :]
            down = work[b, l, j, pl.ds(here - 1, 16), :]
            left = halo[l] if j == 0 else work[b, l, j - 1, pl.ds(here, 16), :]
            right = halo[l] if j == tiles - 1 else work[b, l, j + 1, pl.ds(here, 16), :]
            left = pltpu.roll(jnp.where(lane == 127, left, c), 1, 1)
            right = pltpu.roll(jnp.where(lane == 0, right, c), 127, 1)
            su = cu[l, pl.ds(at, 16), 128 * j : 128 * j + 128].astype(jnp.float32)
            sv = cv[l, pl.ds(at, 16), 128 * j : 128 * j + 128].astype(jnp.float32)
            total = c + jnp.abs(su) * (jnp.where(su > 0, up, down) - c)
            total = total + jnp.abs(sv) * (jnp.where(sv > 0, right, left) - c)
            values.append(total)
        return values

    def run(n, mode):
        source, target = lax.rem(n + 1, 2), lax.rem(n, 2)

        def chunk_of(chunk):
            if mode != "first":
                await_y(n - 1, chunk)
            packed = []
            for m in range(2):
                i = jnp.where(chunk == 0, m * (groups - 1), 2 * chunk - 1 + m)
                at = pl.multiple_of(16 * i, 16)
                here = pl.multiple_of(8 + 16 * i, 8)
                if mode != "first":
                    halo = jnp.where(odd, yrecv[n - 1, 1, chunk], yrecv[n - 1, 0, chunk])
                    halo = [
                        pltpu.roll(halo, (-32 * m - 2 * l) % 128, 1) if m or l else halo
                        for l in range(levels)
                    ]
                kept = []
                for j in range(tiles):
                    if mode == "first":
                        values = [
                            field[l, pl.ds(at, 16), 128 * j : 128 * j + 128]
                            for l in range(levels)
                        ]
                    else:
                        values = moved_by_wind(source, at, here, j, halo)
                    if mode == "last":
                        for l in range(levels):
                            field[l, pl.ds(at, 16), 128 * j : 128 * j + 128] = values[l]
                    else:
                        result = mixed(values, at, j)
                        for l in range(levels):
                            work[target, l, j, pl.ds(here, 16), :] = result[l]
                if mode != "last":
                    ends = [
                        [work[target, l, j, pl.ds(here, 16), :] for l in range(levels)]
                        for j in (0, tiles - 1)
                    ]
                    packed.append(pack(ends[0], ends[1], m))
            if mode != "last":
                ysend[n, chunk] = jnp.where((lane >= 31) & (lane < 63), packed[1], packed[0])
                send_y(n, chunk)

        def edges_first(chunk):
            @pl.when(chunk == 0)
            def _():
                if mode != "first":
                    await_x(n - 1)
                if mode == "middle":
                    @pl.when(n >= 2)
                    def _():
                        await_x_sent(n - 2)

            chunk_of(chunk)
            if mode != "last":
                @pl.when(chunk == 0)
                def _():
                    send_x(n)

        if mode == "middle":
            fori(0, chunks, edges_first)
        else:
            for low, high in zip(bounds, bounds[1:]):
                ready = [p for p, piece in enumerate(pieces) if piece[2] == low]
                if mode == "first":
                    for p in ready:
                        load_f[p].wait()
                        load_k[p].wait()
                fori(low, high, edges_first)
                if mode == "last":
                    for p in ready:
                        saves[p].start()

    run(0, "first")
    fori(1, ny, lambda o: share_y(o).wait_recv())
    fori(1, nx, lambda o: share_x(o).start())
    shared[gx] = held[...]
    for copy in late:
        copy.wait()
    fori(1, ITERS, lambda n: run(n, "middle"))
    run(ITERS, "last")
    fori(1, nx, lambda o: share_x(o).wait_recv())
    fori(1, ny, lambda o: share_y(o).wait_send())
    fori(1, nx, lambda o: share_x(o).wait_send())
    for save in saves:
        save.wait()
    for n in (ITERS - 2, ITERS - 1):
        await_x_sent(n)

    def all_sent(n):
        for side in range(2):
            @pl.when(have_y[side])
            def _():
                fori(0, chunks, lambda chunk: y_copy(n, side, chunk).wait_send())

    fori(0, ITERS, all_sent)


def stencil(f, cu, cv, k, own, nx, ny):
    levels, rows, cols = f.shape
    any_space = pl.BlockSpec(memory_space=pl.ANY)
    vmem = pl.BlockSpec(memory_space=pltpu.VMEM)
    tiles = cols // 128
    chunks = rows // 32
    return pl.pallas_call(
        stencil_kernel,
        out_shape=(
            jax.ShapeDtypeStruct(f.shape, jnp.float32),
            jax.ShapeDtypeStruct((nx, ny, *own.shape), jnp.int32),
        ),
        in_specs=[any_space] * 4 + [vmem],
        out_specs=(any_space, vmem),
        scratch_shapes=[
            pltpu.VMEM(f.shape, jnp.float32),
            pltpu.VMEM(f.shape, jnp.bfloat16),
            pltpu.VMEM(f.shape, jnp.bfloat16),
            pltpu.VMEM(f.shape, jnp.bfloat16),
            pltpu.VMEM((2, levels, tiles, rows + 16, 128), jnp.float32),
            pltpu.VMEM((ITERS, chunks, 16, 128), jnp.float32),
            pltpu.VMEM((ITERS, 2, chunks, 16, 128), jnp.float32),
            pltpu.VMEM((ny, *own.shape), jnp.int32),
            pltpu.SemaphoreType.DMA((3, 4)),
            pltpu.SemaphoreType.DMA((4,)),
            pltpu.SemaphoreType.DMA((ITERS, 2)),
            pltpu.SemaphoreType.DMA((ITERS, 2)),
            pltpu.SemaphoreType.DMA((ITERS, 2, chunks)),
            pltpu.SemaphoreType.DMA((ITERS, 2, chunks)),
            pltpu.SemaphoreType.DMA((ny,)),
            pltpu.SemaphoreType.DMA((ny,)),
            pltpu.SemaphoreType.DMA((nx,)),
            pltpu.SemaphoreType.DMA((nx,)),
        ],
        compiler_params=pltpu.CompilerParams(
            collective_id=0, has_side_effects=True, vmem_limit_bytes=58 * MIB
        ),
        name="stencil",
    )(f, cu, cv, k, own)


def gather_kernel(table, profile, field, out, weights, sums):
    levels = field.shape[0]
    ny, nx = out.shape[0], out.shape[1]
    lane = lax.broadcasted_iota(jnp.int32, (8, 128), 1)
    sub = lax.broadcasted_iota(jnp.int32, (8, 128), 0)

    def spread(r):
        for l in range(levels):
            weights[r, l] = jnp.full((8, 128), profile[r * levels + l], jnp.float32)

    fori(0, profile.shape[0] // levels, spread)

    def weigh(d):
        for h in range(4):
            q = 4 * (4 * d + h)
            row = pl.multiple_of(table[q], 8)
            col = pl.multiple_of(table[q + 1], 128)
            r = table[q + 3]
            terms = [
                weights[r, l] * field[l, pl.ds(row, 8), pl.ds(col, 128)] for l in range(levels)
            ]
            while len(terms) > 1:
                terms = [a + b for a, b in zip(terms[::2], terms[1::2])]
            sums[4 * d + h] = terms[0]

    fori(0, nx * ny, weigh)

    def flatten(c):
        d0 = lax.rem(c, nx // unroll) * unroll, c // (nx // unroll)
        for u in range(unroll):
            g, p = d0[0] + u, d0[1]
            s0 = 4 * (g * ny + p)
            for pair in range(2):
                found = []
                for h in range(2):
                    s = s0 + 2 * pair + h
                    found.append(pltpu.roll(sums[s], table[4 * s + 2], 1))
                both = jnp.where(lane < 64, found[0], found[1])
                for bit in (1, 2, 4):
                    both = jnp.where(sub // bit % 2 == 1, pltpu.roll(both, 8 * bit, 1), both)
                both = jnp.where(lane // 8 % 8 == sub, both, 0.0)
                out[p, g, pair : pair + 1, :] = jnp.sum(both, axis=0, keepdims=True)

    unroll = 4
    fori(0, nx * ny // unroll, flatten)


def gather(table, profile, field, nx, ny):
    smem = pl.BlockSpec(memory_space=pltpu.SMEM)
    vmem = pl.BlockSpec(memory_space=pltpu.VMEM)
    levels = field.shape[0]
    return pl.pallas_call(
        gather_kernel,
        out_shape=jax.ShapeDtypeStruct((ny, nx, 2, 128), jnp.float32),
        in_specs=[smem, smem, vmem],
        out_specs=vmem,
        scratch_shapes=[
            pltpu.VMEM((profile.shape[0] // levels, levels, 8, 128), jnp.float32),
            pltpu.VMEM((4 * nx * ny, 8, 128), jnp.float32),
        ],
        compiler_params=pltpu.CompilerParams(vmem_limit_bytes=24 * MIB),
        name="gather",
    )(table, profile, field)


def exchange_kernel(rows, out, held, send1, recv1, send2, recv2):
    ny, nx = rows.shape[0], rows.shape[1]
    gx, gy = lax.axis_index("gx"), lax.axis_index("gy")
    barrier = pltpu.get_barrier_semaphore()

    def greet_y(o):
        pl.semaphore_signal(
            barrier, inc=1, device_id=(gx, lax.rem(gy + o, ny)), device_id_type=MESH
        )

    def greet_x(o):
        pl.semaphore_signal(
            barrier, inc=1, device_id=(lax.rem(gx + o, nx), gy), device_id_type=MESH
        )

    fori(1, ny, greet_y)
    fori(1, nx, greet_x)
    pl.semaphore_wait(barrier, nx + ny - 2)

    def first(o):
        to = lax.rem(gy + o, ny)
        return pltpu.make_async_remote_copy(
            src_ref=rows.at[to],
            dst_ref=held.at[gy],
            send_sem=send1.at[o],
            recv_sem=recv1.at[o],
            device_id=(gx, to),
            device_id_type=MESH,
        )

    def second(o):
        to = lax.rem(gx + o, nx)
        return pltpu.make_async_remote_copy(
            src_ref=held.at[:, to],
            dst_ref=out.at[gx],
            send_sem=send2.at[o],
            recv_sem=recv2.at[o],
            device_id=(to, gy),
            device_id_type=MESH,
        )

    fori(1, ny, lambda o: first(o).start())
    held[gy] = rows[gy]
    fori(1, ny, lambda o: first(o).wait_recv())
    fori(1, nx, lambda o: second(o).start())
    out[gx] = held[:, gx]
    fori(1, nx, lambda o: second(o).wait_recv())
    fori(1, ny, lambda o: first(o).wait_send())
    fori(1, nx, lambda o: second(o).wait_send())


def exchange(rows):
    ny, nx = rows.shape[0], rows.shape[1]
    vmem = pl.BlockSpec(memory_space=pltpu.VMEM)
    return pl.pallas_call(
        exchange_kernel,
        out_shape=jax.ShapeDtypeStruct((nx, ny, 2, 128), jnp.float32),
        in_specs=[vmem],
        out_specs=vmem,
        scratch_shapes=[
            pltpu.VMEM(rows.shape, jnp.float32),
            pltpu.SemaphoreType.DMA((ny,)),
            pltpu.SemaphoreType.DMA((ny,)),
            pltpu.SemaphoreType.DMA((nx,)),
            pltpu.SemaphoreType.DMA((nx,)),
        ],
        compiler_params=pltpu.CompilerParams(
            collective_id=1, has_side_effects=True, vmem_limit_bytes=16 * MIB
        ),
        name="exchange",
    )(rows)


def gradient_kernel(rows, where, burn, out, column):
    step = pl.program_id(0)
    tiles_dev, width = burn.shape

    @pl.when(step == 0)
    def _():
        values = rows[...]
        high = values.astype(jnp.bfloat16)
        rest = values - high.astype(jnp.float32)
        mid = rest.astype(jnp.bfloat16)
        low = (rest - mid.astype(jnp.float32)).astype(jnp.bfloat16)
        index = where[:, 0:1]
        half = where[:, 1:2]
        count = values.shape[0]
        onehot = (lax.broadcasted_iota(jnp.int32, (tiles_dev, count), 1) == index).astype(
            jnp.float32
        ).astype(jnp.bfloat16)
        lane = lax.broadcasted_iota(jnp.int32, (tiles_dev, 128), 1)
        parts = []
        for part in (high, mid, low):
            picked = jnp.dot(onehot, part, preferred_element_type=jnp.float32)
            parts.append(jnp.where(half == 1, pltpu.roll(picked, 64, 1), picked))
        column[:, 0:128] = jnp.where(lane < 64, parts[0], pltpu.roll(parts[1], 64, 1)).astype(
            jnp.bfloat16
        )
        column[:, 128:256] = jnp.where(lane < 64, parts[2], 0.0).astype(jnp.bfloat16)

    cell = step * width + lax.broadcasted_iota(jnp.int32, (64, width), 1)
    start = SUB * lax.broadcasted_iota(jnp.int32, (64, width), 0)
    spread = ((cell >= start) & (cell < start + SUB)).astype(jnp.float32).astype(jnp.bfloat16)
    spread = jnp.concatenate([spread] * 4, axis=0)
    expanded = jnp.dot(column[...], spread, preferred_element_type=jnp.float32)
    out[...] = (burn[...].astype(jnp.float32) * expanded).astype(jnp.bfloat16)


def gradient(rows, where, burn):
    tiles_dev, fire = burn.shape
    width = 1280
    return pl.pallas_call(
        gradient_kernel,
        grid=(fire // width,),
        out_shape=jax.ShapeDtypeStruct(burn.shape, jnp.bfloat16),
        in_specs=[
            pl.BlockSpec(rows.shape, lambda s: (0, 0)),
            pl.BlockSpec(where.shape, lambda s: (0, 0)),
            pl.BlockSpec((tiles_dev, width), lambda s: (0, s)),
        ],
        out_specs=pl.BlockSpec((tiles_dev, width), lambda s: (0, s)),
        scratch_shapes=[pltpu.VMEM((tiles_dev, 256), jnp.bfloat16)],
        compiler_params=pltpu.CompilerParams(vmem_limit_bytes=24 * MIB),
        name="gradient",
    )(rows, where, burn)


def locate(block_ids, per_x, per_y, blocks_y, gy_count):
    block_row = block_ids // blocks_y
    block_col = block_ids % blocks_y
    source = block_row // per_x * gy_count + block_col // per_y
    local_block = block_row % per_x * per_y + block_col % per_y
    return (source, local_block)


def on_device(
    adjoint_forcing,
    courant_x,
    courant_y,
    vertical_mix,
    tile_block,
    injection_level,
    plume_profile,
    burn_weight,
):
    levels, width_x, width_y = adjoint_forcing.shape
    gx_count = lax.axis_size("gx")
    gy_count = lax.axis_size("gy")
    total = gx_count * gy_count
    tiles_dev = injection_level.shape[0]
    capacity = 4
    per_x = width_x // TB
    per_y = width_y // TB
    blocks_y = per_y * gy_count
    me = lax.axis_index(("gx", "gy"))
    slot_table = tile_block.reshape(total, tiles_dev)
    source, local_block = locate(slot_table, per_x, per_y, blocks_y, gy_count)
    is_mine = (source == me).astype(jnp.int32)
    upto = jnp.triu(jnp.ones((tiles_dev, tiles_dev), jnp.bfloat16))
    rank = jnp.dot(
        is_mine.astype(jnp.bfloat16), upto, preferred_element_type=jnp.float32
    ).astype(jnp.int32) - 1
    slots = jnp.arange(capacity, dtype=jnp.int32)
    hits = (is_mine[:, None, :] == 1) & (rank[:, None, :] == slots[None, :, None])
    local = jnp.sum(jnp.where(hits, local_block[:, None, :], 0), axis=2)
    block_row = local // per_y
    lane_at = local % per_y * TB
    shift = (64 * (slots % 2)[None, :] - lane_at) % 128

    state_field, all_levels = stencil(
        adjoint_forcing, courant_x, courant_y, vertical_mix,
        injection_level.reshape(-1, min(tiles_dev, 128)), gx_count, gy_count,
    )
    all_levels = all_levels.reshape(total, tiles_dev)
    level = jnp.sum(jnp.where(hits, all_levels[:, None, :], 0), axis=2)
    table = jnp.stack(
        [block_row * TB, lane_at // 128 * 128, shift, level], axis=2
    ).reshape(-1)
    rows = gather(table, plume_profile.reshape(-1), state_field, gx_count, gy_count)
    rows = exchange(rows).reshape(total * 2, 128)

    own = lax.dynamic_slice_in_dim(source, me, 1, 0).reshape(tiles_dev)
    positions = jnp.arange(tiles_dev, dtype=jnp.int32)
    earlier = (own[None, :] == own[:, None]) & (positions[None, :] <= positions[:, None])
    arrival = jnp.sum(earlier.astype(jnp.int32), axis=1) - 1
    where = jnp.stack([own * 2 + arrival // 2, arrival % 2], axis=1)
    return (state_field, gradient(rows, where, burn_weight))


def solution(mesh):
    return jax.shard_map(
        on_device,
        mesh=mesh,
        in_specs=(
            P(None, "gx", "gy"),
            P(None, "gx", "gy"),
            P(None, "gx", "gy"),
            P(None, "gx", "gy"),
            P(),
            P(("gx", "gy")),
            P(),
            P(("gx", "gy"), None),
        ),
        out_specs=(P(None, "gx", "gy"), P(("gx", "gy"), None)),
        check_vma=False,
    )
```

```python
import functools

import jax
import jax.numpy as jnp
from jax import lax
from jax.experimental import pallas as pl
from jax.experimental.pallas import tpu as pltpu
from jax.sharding import PartitionSpec as P

ITERS = 4
TB = 8
SUB = 100
MESH = pl.DeviceIdType.MESH
MIB = 1024 * 1024


def fori(low, high, body):
    def step(i, carry):
        body(i)
        return carry

    lax.fori_loop(low, high, step, 0)


def stencil_kernel(
    f_hbm, cu_hbm, cv_hbm, k_hbm, own, table, profile, out, arrived,
    field, cu, cv, mix, work, ysend, yrecv, held, shared, level_of, weights,
    blocks, sums, depart, transit, again,
    load_sem, save_sem, xs_sem, xr_sem, ys_sem, yr_sem,
    send1, recv1, send2, recv2, send3, recv3, send4, recv4, level_sem,
):
    levels, rows, cols = field.shape
    tiles = cols // 128
    groups = rows // 16
    chunks = groups // 2
    early = max(1, (chunks - 1) // 2)
    gx, gy = lax.axis_index("gx"), lax.axis_index("gy")
    nx, ny = lax.axis_size("gx"), lax.axis_size("gy")
    have_x = (gx > 0, gx < nx - 1)
    have_y = (gy > 0, gy < ny - 1)
    peer_x = ((jnp.maximum(gx - 1, 0), gy), (jnp.minimum(gx + 1, nx - 1), gy))
    peer_y = ((gx, jnp.maximum(gy - 1, 0)), (gx, jnp.minimum(gy + 1, ny - 1)))
    lane = lax.broadcasted_iota(jnp.int32, (16, 128), 1)
    odd = lane % 2 == 1

    pieces = [(0, 16, 0), (rows - 16, 16, 0), (16, 32 * early, 1)]
    if chunks - 1 > early:
        pieces.append((16 + 32 * early, 32 * (chunks - 1 - early), 1 + early))
    bounds = sorted({first for _, _, first in pieces}) + [chunks]

    def parts_copy(src, dst, sem):
        return [
            pltpu.make_async_copy(
                src.at[:, pl.ds(at, size), :], dst.at[:, pl.ds(at, size), :], sem.at[p]
            )
            for p, (at, size, _) in enumerate(pieces)
        ]

    load_f = parts_copy(f_hbm, field, load_sem.at[0])
    load_k = parts_copy(k_hbm, mix, load_sem.at[1])
    saves = parts_copy(field, out, save_sem)
    late = [
        pltpu.make_async_copy(cu_hbm, cu, load_sem.at[2, 0]),
        pltpu.make_async_copy(cv_hbm, cv, load_sem.at[2, 1]),
    ]
    for p in range(len(pieces)):
        load_f[p].start()
        load_k[p].start()
    for copy in late:
        copy.start()

    zero_row = jnp.zeros((1, 128), jnp.float32)

    def clear(l):
        for b in range(2):
            for j in range(tiles):
                work[b, l, j, 7:8, :] = zero_row
                work[b, l, j, rows + 8 : rows + 9, :] = zero_row

    fori(0, levels, clear)
    yrecv[...] = jnp.zeros_like(yrecv)

    barrier = pltpu.get_barrier_semaphore()

    def greet_y(o):
        pl.semaphore_signal(
            barrier, inc=1, device_id=(gx, lax.rem(gy + o, ny)), device_id_type=MESH
        )

    def greet_x(o):
        pl.semaphore_signal(
            barrier, inc=1, device_id=(lax.rem(gx + o, nx), gy), device_id_type=MESH
        )

    fori(1, ny, greet_y)
    fori(1, nx, greet_x)
    pl.semaphore_wait(barrier, nx + ny - 2)

    def share_y(o):
        return pltpu.make_async_remote_copy(
            src_ref=own,
            dst_ref=held.at[gy],
            send_sem=send1.at[o],
            recv_sem=recv1.at[o],
            device_id=(gx, lax.rem(gy + o, ny)),
            device_id_type=MESH,
        )

    def share_x(o):
        return pltpu.make_async_remote_copy(
            src_ref=held,
            dst_ref=shared.at[gx],
            send_sem=send2.at[o],
            recv_sem=recv2.at[o],
            device_id=(lax.rem(gx + o, nx), gy),
            device_id_type=MESH,
        )

    fori(1, ny, lambda o: share_y(o).start())
    held[gy] = own[...]

    def x_copy(n, side):
        b = lax.rem(n, 2)
        src, dst = ((8, rows + 8), (rows + 7, 7))[side]
        return pltpu.make_async_remote_copy(
            src_ref=work.at[b, :, :, pl.ds(src, 1), :],
            dst_ref=work.at[b, :, :, pl.ds(dst, 1), :],
            send_sem=xs_sem.at[n, side],
            recv_sem=xr_sem.at[n, side],
            device_id=peer_x[side],
            device_id_type=MESH,
        )

    def y_copy(n, side, chunk):
        return pltpu.make_async_remote_copy(
            src_ref=ysend.at[n, chunk],
            dst_ref=yrecv.at[n, side, chunk],
            send_sem=ys_sem.at[n, side, chunk],
            recv_sem=yr_sem.at[n, side, chunk],
            device_id=peer_y[side],
            device_id_type=MESH,
        )

    def send_x(n):
        for side in range(2):
            @pl.when(have_x[side])
            def _():
                x_copy(n, side).start()

    def send_y(n, chunk):
        for side in range(2):
            @pl.when(have_y[side])
            def _():
                y_copy(n, side, chunk).start()

    def await_x(n):
        for side in range(2):
            @pl.when(have_x[side])
            def _():
                x_copy(n, 1 - side).wait_recv()

    def await_y(n, chunk):
        for side in range(2):
            @pl.when(have_y[side])
            def _():
                y_copy(n, 1 - side, chunk).wait_recv()

    def await_x_sent(n):
        for side in range(2):
            @pl.when(have_x[side])
            def _():
                x_copy(n, side).wait_send()

    def mixed(values, at, j):
        result, before = [], None
        for l in range(levels):
            total = values[l]
            if l < levels - 1:
                k = mix[l, pl.ds(at, 16), 128 * j : 128 * j + 128].astype(jnp.float32)
                flux = k * (values[l + 1] - values[l])
                total = total + flux
            if before is not None:
                total = total - before
            before = flux
            result.append(total)
        return result

    def pack(first, last, m):
        packed = None
        for l in range(levels):
            ends = jnp.where(lane == 0, first[l], last[l])
            if l:
                moved = pltpu.roll(ends, 2 * l, 1)
                packed = jnp.where((lane == 2 * l) | (lane == 2 * l - 1), moved, packed)
            else:
                packed = ends
        return packed if m == 0 else pltpu.roll(packed, 32 * m, 1)

    def moved_by_wind(b, at, here, j, halo):
        values = []
        for l in range(levels):
            c = work[b, l, j, pl.ds(here, 16), :]
            up = work[b, l, j, pl.ds(here + 1, 16), :]
            down = work[b, l, j, pl.ds(here - 1, 16), :]
            left = halo[l] if j == 0 else work[b, l, j - 1, pl.ds(here, 16), :]
            right = halo[l] if j == tiles - 1 else work[b, l, j + 1, pl.ds(here, 16), :]
            left = pltpu.roll(jnp.where(lane == 127, left, c), 1, 1)
            right = pltpu.roll(jnp.where(lane == 0, right, c), 127, 1)
            su = cu[l, pl.ds(at, 16), 128 * j : 128 * j + 128].astype(jnp.float32)
            sv = cv[l, pl.ds(at, 16), 128 * j : 128 * j + 128].astype(jnp.float32)
            total = c + jnp.abs(su) * (jnp.where(su > 0, up, down) - c)
            total = total + jnp.abs(sv) * (jnp.where(sv > 0, right, left) - c)
            values.append(total)
        return values

    def run(n, mode):
        source, target = lax.rem(n + 1, 2), lax.rem(n, 2)

        def chunk_of(chunk):
            if mode != "first":
                await_y(n - 1, chunk)
            packed = []
            for m in range(2):
                i = jnp.where(chunk == 0, m * (groups - 1), 2 * chunk - 1 + m)
                at = pl.multiple_of(16 * i, 16)
                here = pl.multiple_of(8 + 16 * i, 8)
                if mode != "first":
                    halo = jnp.where(odd, yrecv[n - 1, 1, chunk], yrecv[n - 1, 0, chunk])
                    halo = [
                        pltpu.roll(halo, (-32 * m - 2 * l) % 128, 1) if m or l else halo
                        for l in range(levels)
                    ]
                kept = []
                for j in range(tiles):
                    if mode == "first":
                        values = [
                            field[l, pl.ds(at, 16), 128 * j : 128 * j + 128]
                            for l in range(levels)
                        ]
                    else:
                        values = moved_by_wind(source, at, here, j, halo)
                    if mode == "last":
                        for l in range(levels):
                            field[l, pl.ds(at, 16), 128 * j : 128 * j + 128] = values[l]
                            for h in range(2):
                                block = (2 * i + h) * tiles + j
                                blocks[block, l] = values[l][8 * h : 8 * h + 8]
                    else:
                        result = mixed(values, at, j)
                        for l in range(levels):
                            work[target, l, j, pl.ds(here, 16), :] = result[l]
                if mode != "last":
                    ends = [
                        [work[target, l, j, pl.ds(here, 16), :] for l in range(levels)]
                        for j in (0, tiles - 1)
                    ]
                    packed.append(pack(ends[0], ends[1], m))
            if mode != "last":
                ysend[n, chunk] = jnp.where((lane >= 31) & (lane < 63), packed[1], packed[0])
                send_y(n, chunk)

        def edges_first(chunk):
            @pl.when(chunk == 0)
            def _():
                if mode != "first":
                    await_x(n - 1)
                if mode == "middle":
                    @pl.when(n >= 2)
                    def _():
                        await_x_sent(n - 2)

            chunk_of(chunk)
            if mode != "last":
                @pl.when(chunk == 0)
                def _():
                    send_x(n)

        if mode == "middle":
            fori(0, chunks, edges_first)
        else:
            for low, high in zip(bounds, bounds[1:]):
                ready = [p for p, piece in enumerate(pieces) if piece[2] == low]
                if mode == "first":
                    for p in ready:
                        load_f[p].wait()
                        load_k[p].wait()
                fori(low, high, edges_first)
                if mode == "last":
                    for p in ready:
                        saves[p].start()

    run(0, "first")
    fori(1, ny, lambda o: share_y(o).wait_recv())
    fori(1, nx, lambda o: share_x(o).start())
    shared[gx] = held[...]
    for copy in late:
        copy.wait()
    fori(1, ITERS, lambda n: run(n, "middle"))
    fori(1, nx, lambda o: share_x(o).wait_recv())
    to_scalars = pltpu.make_async_copy(shared, level_of, level_sem)
    to_scalars.start()
    run(ITERS, "last")

    def spread(r):
        for l in range(levels):
            weights[r, l] = jnp.full((8, 128), profile[r * levels + l], jnp.float32)

    fori(0, profile.shape[0] // levels, spread)
    to_scalars.wait()

    lane8 = lax.broadcasted_iota(jnp.int32, (8, 128), 1)

    def weigh(p, quad):
        for k in range(16):
            at = 4 * (4 * ((4 * quad + k // 4) * ny + p) + k % 4)
            block = table[at]
            r = level_of[4 * quad + k // 4, p, table[at + 2], table[at + 3]]
            terms = [weights[r, l] * blocks[block, l] for l in range(levels)]
            while len(terms) > 1:
                terms = [a + b for a, b in zip(terms[::2], terms[1::2])]
            sums[quad, k] = jnp.where(lane8 // 8 == table[at + 1], terms[0], 0.0)

    def settle(p):
        lists = [[sums[quad, k] for k in range(16)] for quad in range(nx // 4)]
        for bit in (8, 4, 2, 1):
            low = (lane8 // 8 & bit) == 0
            for quad, found in enumerate(lists):
                folded = []
                for a, b in zip(found[: len(found) // 2], found[len(found) // 2 :]):
                    keep, swap = jnp.where(low, a, b), jnp.where(low, b, a)
                    moved = pltpu.roll(swap, 8 * bit, 1)
                    if bit < 8:
                        moved = jnp.where(low, pltpu.roll(swap, 128 - 8 * bit, 1), moved)
                    folded.append(keep + moved)
                lists[quad] = folded
        for quad, found in enumerate(lists):
            depart[p, quad] = found[0]

    def along_y(o):
        to = lax.rem(gy + o, ny)
        return pltpu.make_async_remote_copy(
            src_ref=depart.at[to],
            dst_ref=transit.at[gy],
            send_sem=send3.at[o],
            recv_sem=recv3.at[o],
            device_id=(gx, to),
            device_id_type=MESH,
        )

    def along_x(o):
        to = lax.rem(gx + o, nx)
        return pltpu.make_async_remote_copy(
            src_ref=again.at[to],
            dst_ref=arrived.at[gx],
            send_sem=send4.at[o],
            recv_sem=recv4.at[o],
            device_id=(to, gy),
            device_id_type=MESH,
        )

    def depart_to(o):
        p = lax.rem(gy + o, ny)
        fori(0, nx // 4, lambda quad: weigh(p, quad))
        settle(p)

        @pl.when(o < ny)
        def _():
            along_y(o).start()

    fori(1, ny + 1, depart_to)
    transit[gy] = depart[gy]
    fori(1, ny, lambda o: along_y(o).wait_recv())

    def pass_on(quad):
        for u in range(4):
            for h in range(again.shape[1]):
                packed = None
                for j in range(min(ny, 4)):
                    moved = transit[4 * h + j, quad]
                    if j != u:
                        moved = pltpu.roll(moved, 32 * (j - u) % 128, 1)
                    packed = moved if j == 0 else jnp.where(lane8 // 32 == j, moved, packed)
                again[4 * quad + u, h] = packed
            o = lax.rem(4 * quad + u + nx - gx, nx)

            @pl.when(o > 0)
            def _():
                along_x(o).start()

    fori(0, nx // 4, pass_on)
    arrived[gx] = again[gx]
    fori(1, nx, lambda o: along_x(o).wait_recv())
    fori(1, ny, lambda o: along_y(o).wait_send())
    fori(1, nx, lambda o: along_x(o).wait_send())
    fori(1, ny, lambda o: share_y(o).wait_send())
    fori(1, nx, lambda o: share_x(o).wait_send())
    for save in saves:
        save.wait()
    for n in (ITERS - 2, ITERS - 1):
        await_x_sent(n)

    def all_sent(n):
        for side in range(2):
            @pl.when(have_y[side])
            def _():
                fori(0, chunks, lambda chunk: y_copy(n, side, chunk).wait_send())

    fori(0, ITERS, all_sent)


def stencil(f, cu, cv, k, own, table, profile, nx, ny):
    levels, rows, cols = f.shape
    any_space = pl.BlockSpec(memory_space=pl.ANY)
    vmem = pl.BlockSpec(memory_space=pltpu.VMEM)
    tiles = cols // 128
    chunks = rows // 32
    smem = pl.BlockSpec(memory_space=pltpu.SMEM)
    halves = max(1, ny // 4)
    return pl.pallas_call(
        stencil_kernel,
        out_shape=(
            jax.ShapeDtypeStruct(f.shape, jnp.float32),
            jax.ShapeDtypeStruct((nx, halves, 8, 128), jnp.float32),
        ),
        in_specs=[any_space] * 4 + [vmem, smem, smem],
        out_specs=(any_space, vmem),
        scratch_shapes=[
            pltpu.VMEM(f.shape, jnp.float32),
            pltpu.VMEM(f.shape, jnp.bfloat16),
            pltpu.VMEM(f.shape, jnp.bfloat16),
            pltpu.VMEM(f.shape, jnp.bfloat16),
            pltpu.VMEM((2, levels, tiles, rows + 16, 128), jnp.float32),
            pltpu.VMEM((ITERS, chunks, 16, 128), jnp.float32),
            pltpu.VMEM((ITERS, 2, chunks, 16, 128), jnp.float32),
            pltpu.VMEM((ny, *own.shape), jnp.int32),
            pltpu.VMEM((nx, ny, *own.shape), jnp.int32),
            pltpu.SMEM((nx, ny, *own.shape), jnp.int32),
            pltpu.VMEM((profile.shape[0] // levels, levels, 8, 128), jnp.float32),
            pltpu.VMEM((rows // 8 * tiles, levels, 8, 128), jnp.float32),
            pltpu.VMEM((nx // 4, 16, 8, 128), jnp.float32),
            pltpu.VMEM((ny, nx // 4, 8, 128), jnp.float32),
            pltpu.VMEM((ny, nx // 4, 8, 128), jnp.float32),
            pltpu.VMEM((nx, halves, 8, 128), jnp.float32),
            pltpu.SemaphoreType.DMA((3, 4)),
            pltpu.SemaphoreType.DMA((4,)),
            pltpu.SemaphoreType.DMA((ITERS, 2)),
            pltpu.SemaphoreType.DMA((ITERS, 2)),
            pltpu.SemaphoreType.DMA((ITERS, 2, chunks)),
            pltpu.SemaphoreType.DMA((ITERS, 2, chunks)),
            pltpu.SemaphoreType.DMA((ny,)),
            pltpu.SemaphoreType.DMA((ny,)),
            pltpu.SemaphoreType.DMA((nx,)),
            pltpu.SemaphoreType.DMA((nx,)),
            pltpu.SemaphoreType.DMA((ny,)),
            pltpu.SemaphoreType.DMA((ny,)),
            pltpu.SemaphoreType.DMA((nx,)),
            pltpu.SemaphoreType.DMA((nx,)),
            pltpu.SemaphoreType.DMA,
        ],
        compiler_params=pltpu.CompilerParams(
            collective_id=0, has_side_effects=True, vmem_limit_bytes=58 * MIB
        ),
        name="stencil",
    )(f, cu, cv, k, own, table, profile)


def gradient_kernel(rows, where, burn, state, out, state_out, column, held, copy_sem):
    step = pl.program_id(0)
    part = state.shape[0] // 4
    loads, saves = [], []
    for i in range(4):
        at = pl.ds(part * i, part)
        loads.append(pltpu.make_async_copy(state.at[at], held.at[at], copy_sem.at[0, i]))
        saves.append(pltpu.make_async_copy(held.at[at], state_out.at[at], copy_sem.at[1, i]))
    tiles_dev, width = burn.shape

    @pl.when(step == 0)
    def _():
        for load in loads:
            load.start()
        values = rows[...]
        sub = lax.broadcasted_iota(jnp.int32, values.shape, 1)
        group = lax.broadcasted_iota(jnp.int32, values.shape, 2) // 8
        for bit in (1, 2, 4):
            low = pltpu.roll(pltpu.roll(values, 8 - bit, 1), 8 * bit, 2)
            high = pltpu.roll(pltpu.roll(values, bit, 1), 128 - 8 * bit, 2)
            in_row, in_group = sub // bit % 2, group // bit % 2
            values = jnp.where(
                in_row == in_group, values, jnp.where(in_group == 1, low, high)
            )
        values = values.reshape(-1, 128)
        high = values.astype(jnp.bfloat16)
        rest = values - high.astype(jnp.float32)
        mid = rest.astype(jnp.bfloat16)
        low = (rest - mid.astype(jnp.float32)).astype(jnp.bfloat16)
        index = where[:, 0:1]
        half = where[:, 1:2]
        count = values.shape[0]
        onehot = (lax.broadcasted_iota(jnp.int32, (tiles_dev, count), 1) == index).astype(
            jnp.float32
        ).astype(jnp.bfloat16)
        lane = lax.broadcasted_iota(jnp.int32, (tiles_dev, 128), 1)
        parts = []
        for part in (high, mid, low):
            picked = jnp.dot(onehot, part, preferred_element_type=jnp.float32)
            parts.append(jnp.where(half == 1, pltpu.roll(picked, 64, 1), picked))
        column[:, 0:128] = jnp.where(lane < 64, parts[0], pltpu.roll(parts[1], 64, 1)).astype(
            jnp.bfloat16
        )
        column[:, 128:256] = jnp.where(lane < 64, parts[2], 0.0).astype(jnp.bfloat16)

    cell = step * width + lax.broadcasted_iota(jnp.int32, (64, width), 1)
    start = SUB * lax.broadcasted_iota(jnp.int32, (64, width), 0)
    spread = ((cell >= start) & (cell < start + SUB)).astype(jnp.float32).astype(jnp.bfloat16)
    spread = jnp.concatenate([spread] * 4, axis=0)
    expanded = jnp.dot(column[...], spread, preferred_element_type=jnp.float32)
    out[...] = (burn[...].astype(jnp.float32) * expanded).astype(jnp.bfloat16)

    for i in range(4):
        @pl.when(step == i)
        def _():
            loads[i].wait()
            saves[i].start()

    @pl.when(step == pl.num_programs(0) - 1)
    def _():
        for save in saves:
            save.wait()


def gradient(rows, where, burn, state):
    tiles_dev, fire = burn.shape
    width = 1280
    return pl.pallas_call(
        gradient_kernel,
        grid=(fire // width,),
        out_shape=(
            jax.ShapeDtypeStruct(burn.shape, jnp.bfloat16),
            jax.ShapeDtypeStruct(state.shape, state.dtype),
        ),
        in_specs=[
            pl.BlockSpec(rows.shape, lambda s: (0, 0, 0)),
            pl.BlockSpec(where.shape, lambda s: (0, 0)),
            pl.BlockSpec((tiles_dev, width), lambda s: (0, s)),
            pl.BlockSpec(memory_space=pl.ANY),
        ],
        out_specs=(
            pl.BlockSpec((tiles_dev, width), lambda s: (0, s)),
            pl.BlockSpec(memory_space=pl.ANY),
        ),
        scratch_shapes=[
            pltpu.VMEM((tiles_dev, 256), jnp.bfloat16),
            pltpu.VMEM(state.shape, state.dtype),
            pltpu.SemaphoreType.DMA((2, 4)),
        ],
        compiler_params=pltpu.CompilerParams(vmem_limit_bytes=50 * MIB),
        name="gradient",
    )(rows, where, burn, state)


def locate(block_ids, per_x, per_y, blocks_y, gy_count):
    block_row = block_ids // blocks_y
    block_col = block_ids % blocks_y
    source = block_row // per_x * gy_count + block_col // per_y
    local_block = block_row % per_x * per_y + block_col % per_y
    return (source, local_block)


def on_device(
    adjoint_forcing,
    courant_x,
    courant_y,
    vertical_mix,
    tile_block,
    injection_level,
    plume_profile,
    burn_weight,
):
    levels, width_x, width_y = adjoint_forcing.shape
    gx_count = lax.axis_size("gx")
    gy_count = lax.axis_size("gy")
    total = gx_count * gy_count
    tiles_dev = injection_level.shape[0]
    capacity = 4
    per_x = width_x // TB
    per_y = width_y // TB
    blocks_y = per_y * gy_count
    me = lax.axis_index(("gx", "gy"))
    slot_table = tile_block.reshape(total, tiles_dev)
    source, local_block = locate(slot_table, per_x, per_y, blocks_y, gy_count)
    is_mine = (source == me).astype(jnp.int32)
    upto = jnp.triu(jnp.ones((tiles_dev, tiles_dev), jnp.bfloat16))
    rank = jnp.dot(
        is_mine.astype(jnp.bfloat16), upto, preferred_element_type=jnp.float32
    ).astype(jnp.int32) - 1
    slots = jnp.arange(capacity, dtype=jnp.int32)
    hits = (is_mine[:, None, :] == 1) & (rank[:, None, :] == slots[None, :, None])
    local = jnp.sum(jnp.where(hits, local_block[:, None, :], 0), axis=2)
    block_row = local // per_y
    lane_at = local % per_y * TB
    place = jnp.sum(jnp.where(hits, jnp.arange(tiles_dev, dtype=jnp.int32), 0), axis=2)
    share = min(tiles_dev, 128)
    table = jnp.stack(
        [
            block_row * (width_y // 128) + lane_at // 128,
            lane_at % 128 // TB,
            place // share,
            place % share,
        ],
        axis=2,
    ).reshape(-1)

    state_field, rows = stencil(
        adjoint_forcing, courant_x, courant_y, vertical_mix,
        injection_level.reshape(-1, share), table, plume_profile.reshape(-1),
        gx_count, gy_count,
    )
    rows = rows.reshape(-1, 8, 128)

    own = lax.dynamic_slice_in_dim(source, me, 1, 0).reshape(tiles_dev)
    positions = jnp.arange(tiles_dev, dtype=jnp.int32)
    earlier = (own[None, :] == own[:, None]) & (positions[None, :] <= positions[:, None])
    arrival = jnp.sum(earlier.astype(jnp.int32), axis=1) - 1
    far, near = own // gy_count, own % gy_count
    spot = near % 4 * 4 + arrival
    row = (far * max(1, gy_count // 4) + near // 4) * 8 + spot % 8
    where = jnp.stack([row, spot // 8], axis=1)
    gradient_out, state_out = gradient(rows, where, burn_weight, state_field)
    return (state_out, gradient_out)


def solution(mesh):
    return jax.shard_map(
        on_device,
        mesh=mesh,
        in_specs=(
            P(None, "gx", "gy"),
            P(None, "gx", "gy"),
            P(None, "gx", "gy"),
            P(None, "gx", "gy"),
            P(),
            P(("gx", "gy")),
            P(),
            P(("gx", "gy"), None),
        ),
        out_specs=(P(None, "gx", "gy"), P(("gx", "gy"), None)),
        check_vma=False,
    )
```

```python
import functools

import jax
import jax.numpy as jnp
from jax import lax
from jax.experimental import pallas as pl
from jax.experimental.pallas import tpu as pltpu
from jax.sharding import PartitionSpec as P

ITERS = 4
TB = 8
SUB = 100
MESH = pl.DeviceIdType.MESH
MIB = 1024 * 1024


def fori(low, high, body):
    def step(i, carry):
        body(i)
        return carry

    lax.fori_loop(low, high, step, 0)


def stencil_kernel(
    f_hbm, cu_hbm, cv_hbm, k_hbm, own, table, profile, out, arrived,
    field, cu, cv, mix, work0, work1, ysend, yrecv, held, shared, level_of, weights,
    blocks, sums, depart, transit, again,
    load_sem, save_sem, xs_sem, xr_sem, ys_sem, yr_sem,
    send1, recv1, send2, recv2, send3, recv3, send4, recv4, level_sem,
):
    levels, rows, cols = field.shape
    tiles = cols // 128
    groups = rows // 16
    chunks = groups // 4
    work = (work0, work1)
    gx, gy = lax.axis_index("gx"), lax.axis_index("gy")
    nx, ny = lax.axis_size("gx"), lax.axis_size("gy")
    have_x = (gx > 0, gx < nx - 1)
    have_y = (gy > 0, gy < ny - 1)
    peer_x = ((jnp.maximum(gx - 1, 0), gy), (jnp.minimum(gx + 1, nx - 1), gy))
    peer_y = ((gx, jnp.maximum(gy - 1, 0)), (gx, jnp.minimum(gy + 1, ny - 1)))
    lane = lax.broadcasted_iota(jnp.int32, (16, 128), 1)
    odd = lane % 2 == 1

    pieces = [(0, 48, 0), (rows - 16, 16, 0)]
    pieces += [(64 * c - 16, 64, c) for c in range(1, chunks)]
    bounds = list(range(chunks + 1))

    def parts_copy(src, dst, sem):
        return [
            pltpu.make_async_copy(
                src.at[:, pl.ds(at, size), :], dst.at[:, pl.ds(at, size), :], sem.at[p]
            )
            for p, (at, size, _) in enumerate(pieces)
        ]

    load_f = parts_copy(f_hbm, field, load_sem.at[0])
    load_k = parts_copy(k_hbm, mix, load_sem.at[1])
    saves = parts_copy(field, out, save_sem)
    late = [
        pltpu.make_async_copy(cu_hbm, cu, load_sem.at[2, 0]),
        pltpu.make_async_copy(cv_hbm, cv, load_sem.at[2, 1]),
    ]
    for p in range(len(pieces)):
        load_f[p].start()
        load_k[p].start()
    for copy in late:
        copy.start()

    zero_row = jnp.zeros((1, 128), jnp.float32)

    def clear(l):
        for b in range(2):
            for j in range(tiles):
                work[b][l, j, 7:8, :] = zero_row
                work[b][l, j, rows + 8 : rows + 9, :] = zero_row

    fori(0, levels, clear)
    yrecv[...] = jnp.zeros_like(yrecv)

    barrier = pltpu.get_barrier_semaphore()

    def greet_y(o):
        pl.semaphore_signal(
            barrier, inc=1, device_id=(gx, lax.rem(gy + o, ny)), device_id_type=MESH
        )

    def greet_x(o):
        pl.semaphore_signal(
            barrier, inc=1, device_id=(lax.rem(gx + o, nx), gy), device_id_type=MESH
        )

    fori(1, ny, greet_y)
    fori(1, nx, greet_x)
    pl.semaphore_wait(barrier, nx + ny - 2)

    def share_y(o):
        return pltpu.make_async_remote_copy(
            src_ref=own,
            dst_ref=held.at[gy],
            send_sem=send1.at[o],
            recv_sem=recv1.at[o],
            device_id=(gx, lax.rem(gy + o, ny)),
            device_id_type=MESH,
        )

    def share_x(o):
        return pltpu.make_async_remote_copy(
            src_ref=held,
            dst_ref=shared.at[gx],
            send_sem=send2.at[o],
            recv_sem=recv2.at[o],
            device_id=(lax.rem(gx + o, nx), gy),
            device_id_type=MESH,
        )

    fori(1, ny, lambda o: share_y(o).start())
    held[gy] = own[...]

    def x_copy(n, side):
        b = n % 2
        src, dst = ((8, rows + 8), (rows + 7, 7))[side]
        return pltpu.make_async_remote_copy(
            src_ref=work[b].at[:, :, pl.ds(src, 1), :],
            dst_ref=work[b].at[:, :, pl.ds(dst, 1), :],
            send_sem=xs_sem.at[n, side],
            recv_sem=xr_sem.at[n, side],
            device_id=peer_x[side],
            device_id_type=MESH,
        )

    def y_copy(n, side, chunk):
        return pltpu.make_async_remote_copy(
            src_ref=ysend.at[n, chunk],
            dst_ref=yrecv.at[n, side, chunk],
            send_sem=ys_sem.at[n, side, chunk],
            recv_sem=yr_sem.at[n, side, chunk],
            device_id=peer_y[side],
            device_id_type=MESH,
        )

    def send_x(n):
        for side in range(2):
            @pl.when(have_x[side])
            def _():
                x_copy(n, side).start()

    def send_y(n, chunk):
        for side in range(2):
            @pl.when(have_y[side])
            def _():
                y_copy(n, side, chunk).start()

    def await_x(n):
        for side in range(2):
            @pl.when(have_x[side])
            def _():
                x_copy(n, 1 - side).wait_recv()

    def await_y(n, chunk):
        for side in range(2):
            @pl.when(have_y[side])
            def _():
                y_copy(n, 1 - side, chunk).wait_recv()

    def await_x_sent(n):
        for side in range(2):
            @pl.when(have_x[side])
            def _():
                x_copy(n, side).wait_send()

    def mixed(values, at, j):
        result, before = [], None
        for l in range(levels):
            total = values[l]
            if l < levels - 1:
                k = mix[l, pl.ds(at, 16), 128 * j : 128 * j + 128].astype(jnp.float32)
                flux = k * (values[l + 1] - values[l])
                total = total + flux
            if before is not None:
                total = total - before
            before = flux
            result.append(total)
        return result

    def pack(first, last, m):
        packed = None
        for l in range(levels):
            ends = jnp.where(lane == 0, first[l], last[l])
            if l:
                moved = pltpu.roll(ends, 2 * l, 1)
                packed = jnp.where((lane == 2 * l) | (lane == 2 * l - 1), moved, packed)
            else:
                packed = ends
        return packed if m == 0 else pltpu.roll(packed, 32 * m, 1)

    def moved_by_wind(b, at, here, j, halo):
        values = []
        for l in range(levels):
            c = work[b][l, j, pl.ds(here, 16), :]
            up = work[b][l, j, pl.ds(here + 1, 16), :]
            down = work[b][l, j, pl.ds(here - 1, 16), :]
            left = halo[l] if j == 0 else work[b][l, j - 1, pl.ds(here, 16), :]
            right = halo[l] if j == tiles - 1 else work[b][l, j + 1, pl.ds(here, 16), :]
            left = pltpu.roll(jnp.where(lane == 127, left, c), 1, 1)
            right = pltpu.roll(jnp.where(lane == 0, right, c), 127, 1)
            su = cu[l, pl.ds(at, 16), 128 * j : 128 * j + 128].astype(jnp.float32)
            sv = cv[l, pl.ds(at, 16), 128 * j : 128 * j + 128].astype(jnp.float32)
            total = c + jnp.abs(su) * (jnp.where(su > 0, up, down) - c)
            total = total + jnp.abs(sv) * (jnp.where(sv > 0, right, left) - c)
            values.append(total)
        return values

    def run(n, mode):
        source, target = (n + 1) % 2, n % 2

        def chunk_of(chunk):
            if mode != "first":
                await_y(n - 1, chunk)
            packed = []
            for m in range(4):
                i = jnp.where(chunk == 0, (0, groups - 1, 1, 2)[m], 4 * chunk - 1 + m)
                at = pl.multiple_of(16 * i, 16)
                here = pl.multiple_of(8 + 16 * i, 8)
                if mode != "first":
                    halo = jnp.where(odd, yrecv[n - 1, 1, chunk], yrecv[n - 1, 0, chunk])
                    halo = [
                        pltpu.roll(halo, (-32 * m - 2 * l) % 128, 1) if m or l else halo
                        for l in range(levels)
                    ]
                kept = []
                for j in range(tiles):
                    if mode == "first":
                        values = [
                            field[l, pl.ds(at, 16), 128 * j : 128 * j + 128]
                            for l in range(levels)
                        ]
                    else:
                        values = moved_by_wind(source, at, here, j, halo)
                    if mode == "last":
                        for l in range(levels):
                            field[l, pl.ds(at, 16), 128 * j : 128 * j + 128] = values[l]
                            for h in range(2):
                                block = (2 * i + h) * tiles + j
                                blocks[block, l] = values[l][8 * h : 8 * h + 8]
                    else:
                        result = mixed(values, at, j)
                        for l in range(levels):
                            work[target][l, j, pl.ds(here, 16), :] = result[l]
                if mode != "last":
                    ends = [
                        [work[target][l, j, pl.ds(here, 16), :] for l in range(levels)]
                        for j in (0, tiles - 1)
                    ]
                    packed.append(pack(ends[0], ends[1], m))
            if mode != "last":
                ends = packed[0]
                for m in range(1, 4):
                    ends = jnp.where((lane >= 32 * m - 1) & (lane < 32 * m + 31), packed[m], ends)
                ysend[n, chunk] = ends
                send_y(n, chunk)

        def edges_first(chunk):
            @pl.when(chunk == 0)
            def _():
                if mode != "first":
                    await_x(n - 1)
                if mode == "middle" and n >= 2:
                    await_x_sent(n - 2)

            chunk_of(chunk)
            if mode != "last":
                @pl.when(chunk == 0)
                def _():
                    send_x(n)

        if mode == "middle":
            fori(0, chunks, edges_first)
        else:
            for low, high in zip(bounds, bounds[1:]):
                ready = [p for p, piece in enumerate(pieces) if piece[2] == low]
                if mode == "first":
                    for p in ready:
                        load_f[p].wait()
                        load_k[p].wait()
                fori(low, high, edges_first)
                if mode == "last":
                    for p in ready:
                        saves[p].start()

    run(0, "first")
    fori(1, ny, lambda o: share_y(o).wait_recv())
    fori(1, nx, lambda o: share_x(o).start())
    shared[gx] = held[...]
    for copy in late:
        copy.wait()
    for n in range(1, ITERS):
        run(n, "middle")
    fori(1, nx, lambda o: share_x(o).wait_recv())
    to_scalars = pltpu.make_async_copy(shared, level_of, level_sem)
    to_scalars.start()
    run(ITERS, "last")

    def spread(r):
        for l in range(levels):
            weights[r, l] = jnp.full((8, 128), profile[r, l], jnp.float32)

    fori(0, profile.shape[0], spread)
    to_scalars.wait()

    lane8 = lax.broadcasted_iota(jnp.int32, (8, 128), 1)

    def weigh(p, quad):
        for k in range(16):
            g = 4 * quad + k // 4
            block, lanes, high, low = (table[4 * a + k % 4, g * ny + p] for a in range(4))
            r = level_of[g, p, high, low]
            terms = [weights[r, l] * blocks[block, l] for l in range(levels)]
            while len(terms) > 1:
                terms = [a + b for a, b in zip(terms[::2], terms[1::2])]
            sums[quad, k] = jnp.where(lane8 // 8 == lanes, terms[0], 0.0)

    def settle(p):
        lists = [[sums[quad, k] for k in range(16)] for quad in range(nx // 4)]
        for bit in (8, 4, 2, 1):
            low = (lane8 // 8 & bit) == 0
            for quad, found in enumerate(lists):
                folded = []
                for a, b in zip(found[: len(found) // 2], found[len(found) // 2 :]):
                    keep, swap = jnp.where(low, a, b), jnp.where(low, b, a)
                    moved = pltpu.roll(swap, 8 * bit, 1)
                    if bit < 8:
                        moved = jnp.where(low, pltpu.roll(swap, 128 - 8 * bit, 1), moved)
                    folded.append(keep + moved)
                lists[quad] = folded
        for quad, found in enumerate(lists):
            depart[p, quad] = found[0]

    def along_y(o):
        to = lax.rem(gy + o, ny)
        return pltpu.make_async_remote_copy(
            src_ref=depart.at[to],
            dst_ref=transit.at[gy],
            send_sem=send3.at[o],
            recv_sem=recv3.at[o],
            device_id=(gx, to),
            device_id_type=MESH,
        )

    def along_x(o):
        to = lax.rem(gx + o, nx)
        return pltpu.make_async_remote_copy(
            src_ref=again.at[to],
            dst_ref=arrived.at[gx],
            send_sem=send4.at[o],
            recv_sem=recv4.at[o],
            device_id=(to, gy),
            device_id_type=MESH,
        )

    def depart_to(o):
        p = lax.rem(gy + o, ny)
        fori(0, nx // 4, lambda quad: weigh(p, quad))
        settle(p)

        @pl.when(o < ny)
        def _():
            along_y(o).start()

    fori(1, ny + 1, depart_to)
    transit[gy] = depart[gy]
    fori(1, ny, lambda o: along_y(o).wait_recv())

    def pass_on(quad):
        for u in range(4):
            for h in range(again.shape[1]):
                packed = None
                for j in range(min(ny, 4)):
                    moved = transit[4 * h + j, quad]
                    if j != u:
                        moved = pltpu.roll(moved, 32 * (j - u) % 128, 1)
                    packed = moved if j == 0 else jnp.where(lane8 // 32 == j, moved, packed)
                again[4 * quad + u, h] = packed
            o = lax.rem(4 * quad + u + nx - gx, nx)

            @pl.when(o > 0)
            def _():
                along_x(o).start()

    fori(0, nx // 4, pass_on)
    arrived[gx] = again[gx]
    fori(1, nx, lambda o: along_x(o).wait_recv())
    fori(1, ny, lambda o: along_y(o).wait_send())
    fori(1, nx, lambda o: along_x(o).wait_send())
    fori(1, ny, lambda o: share_y(o).wait_send())
    fori(1, nx, lambda o: share_x(o).wait_send())
    for save in saves:
        save.wait()
    for n in (ITERS - 2, ITERS - 1):
        await_x_sent(n)

    def all_sent(n):
        for side in range(2):
            @pl.when(have_y[side])
            def _():
                fori(0, chunks, lambda chunk: y_copy(n, side, chunk).wait_send())

    fori(0, ITERS, all_sent)


def stencil(f, cu, cv, k, own, table, profile, nx, ny):
    levels, rows, cols = f.shape
    any_space = pl.BlockSpec(memory_space=pl.ANY)
    vmem = pl.BlockSpec(memory_space=pltpu.VMEM)
    tiles = cols // 128
    chunks = rows // 64
    smem = pl.BlockSpec(memory_space=pltpu.SMEM)
    halves = max(1, ny // 4)
    return pl.pallas_call(
        stencil_kernel,
        out_shape=(
            jax.ShapeDtypeStruct(f.shape, jnp.float32),
            jax.ShapeDtypeStruct((nx, halves, 8, 128), jnp.float32),
        ),
        in_specs=[any_space] * 4 + [vmem, smem, smem],
        out_specs=(any_space, vmem),
        scratch_shapes=[
            pltpu.VMEM(f.shape, jnp.float32),
            pltpu.VMEM(f.shape, jnp.bfloat16),
            pltpu.VMEM(f.shape, jnp.bfloat16),
            pltpu.VMEM(f.shape, jnp.bfloat16),
            pltpu.VMEM((levels, tiles, rows + 16, 128), jnp.float32),
            pltpu.VMEM((levels, tiles, rows + 16, 128), jnp.float32),
            pltpu.VMEM((ITERS, chunks, 16, 128), jnp.float32),
            pltpu.VMEM((ITERS, 2, chunks, 16, 128), jnp.float32),
            pltpu.VMEM((ny, *own.shape), jnp.int32),
            pltpu.VMEM((nx, ny, *own.shape), jnp.int32),
            pltpu.SMEM((nx, ny, *own.shape), jnp.int32),
            pltpu.VMEM((*profile.shape, 8, 128), jnp.float32),
            pltpu.VMEM((rows // 8 * tiles, levels, 8, 128), jnp.float32),
            pltpu.VMEM((nx // 4, 16, 8, 128), jnp.float32),
            pltpu.VMEM((ny, nx // 4, 8, 128), jnp.float32),
            pltpu.VMEM((ny, nx // 4, 8, 128), jnp.float32),
            pltpu.VMEM((nx, halves, 8, 128), jnp.float32),
            pltpu.SemaphoreType.DMA((3, 4)),
            pltpu.SemaphoreType.DMA((4,)),
            pltpu.SemaphoreType.DMA((ITERS, 2)),
            pltpu.SemaphoreType.DMA((ITERS, 2)),
            pltpu.SemaphoreType.DMA((ITERS, 2, chunks)),
            pltpu.SemaphoreType.DMA((ITERS, 2, chunks)),
            pltpu.SemaphoreType.DMA((ny,)),
            pltpu.SemaphoreType.DMA((ny,)),
            pltpu.SemaphoreType.DMA((nx,)),
            pltpu.SemaphoreType.DMA((nx,)),
            pltpu.SemaphoreType.DMA((ny,)),
            pltpu.SemaphoreType.DMA((ny,)),
            pltpu.SemaphoreType.DMA((nx,)),
            pltpu.SemaphoreType.DMA((nx,)),
            pltpu.SemaphoreType.DMA,
        ],
        compiler_params=pltpu.CompilerParams(
            collective_id=0, has_side_effects=True, vmem_limit_bytes=58 * MIB
        ),
        name="stencil",
    )(f, cu, cv, k, own, table, profile)


def gradient_kernel(rows, where, burn, state, out, state_out, column, held, copy_sem):
    step = pl.program_id(0)
    part = state.shape[0] // 4
    loads, saves = [], []
    for i in range(4):
        at = pl.ds(part * i, part)
        loads.append(pltpu.make_async_copy(state.at[at], held.at[at], copy_sem.at[0, i]))
        saves.append(pltpu.make_async_copy(held.at[at], state_out.at[at], copy_sem.at[1, i]))
    tiles_dev, width = burn.shape

    @pl.when(step == 0)
    def _():
        for load in loads:
            load.start()
        values = rows[...]
        sub = lax.broadcasted_iota(jnp.int32, values.shape, 1)
        group = lax.broadcasted_iota(jnp.int32, values.shape, 2) // 8
        for bit in (1, 2, 4):
            low = pltpu.roll(pltpu.roll(values, 8 - bit, 1), 8 * bit, 2)
            high = pltpu.roll(pltpu.roll(values, bit, 1), 128 - 8 * bit, 2)
            in_row, in_group = sub // bit % 2, group // bit % 2
            values = jnp.where(
                in_row == in_group, values, jnp.where(in_group == 1, low, high)
            )
        values = values.reshape(-1, 128)
        high = values.astype(jnp.bfloat16)
        rest = values - high.astype(jnp.float32)
        mid = rest.astype(jnp.bfloat16)
        low = (rest - mid.astype(jnp.float32)).astype(jnp.bfloat16)
        index = where[:, 0:1]
        half = where[:, 1:2]
        count = values.shape[0]
        onehot = (lax.broadcasted_iota(jnp.int32, (tiles_dev, count), 1) == index).astype(
            jnp.float32
        ).astype(jnp.bfloat16)
        lane = lax.broadcasted_iota(jnp.int32, (tiles_dev, 128), 1)
        parts = []
        for part in (high, mid, low):
            picked = jnp.dot(onehot, part, preferred_element_type=jnp.float32)
            parts.append(jnp.where(half == 1, pltpu.roll(picked, 64, 1), picked))
        column[:, 0:128] = jnp.where(lane < 64, parts[0], pltpu.roll(parts[1], 64, 1)).astype(
            jnp.bfloat16
        )
        column[:, 128:256] = jnp.where(lane < 64, parts[2], 0.0).astype(jnp.bfloat16)

    cell = step * width + lax.broadcasted_iota(jnp.int32, (64, width), 1)
    start = SUB * lax.broadcasted_iota(jnp.int32, (64, width), 0)
    spread = ((cell >= start) & (cell < start + SUB)).astype(jnp.float32).astype(jnp.bfloat16)
    spread = jnp.concatenate([spread] * 4, axis=0)
    expanded = jnp.dot(column[...], spread, preferred_element_type=jnp.float32)
    out[...] = (burn[...].astype(jnp.float32) * expanded).astype(jnp.bfloat16)

    for i in range(4):
        @pl.when(step == i)
        def _():
            loads[i].wait()
            saves[i].start()

    @pl.when(step == pl.num_programs(0) - 1)
    def _():
        for save in saves:
            save.wait()


def gradient(rows, where, burn, state):
    tiles_dev, fire = burn.shape
    width = 1280
    return pl.pallas_call(
        gradient_kernel,
        grid=(fire // width,),
        out_shape=(
            jax.ShapeDtypeStruct(burn.shape, jnp.bfloat16),
            jax.ShapeDtypeStruct(state.shape, state.dtype),
        ),
        in_specs=[
            pl.BlockSpec(rows.shape, lambda s: (0, 0, 0)),
            pl.BlockSpec(where.shape, lambda s: (0, 0)),
            pl.BlockSpec((tiles_dev, width), lambda s: (0, s)),
            pl.BlockSpec(memory_space=pl.ANY),
        ],
        out_specs=(
            pl.BlockSpec((tiles_dev, width), lambda s: (0, s)),
            pl.BlockSpec(memory_space=pl.ANY),
        ),
        scratch_shapes=[
            pltpu.VMEM((tiles_dev, 256), jnp.bfloat16),
            pltpu.VMEM(state.shape, state.dtype),
            pltpu.SemaphoreType.DMA((2, 4)),
        ],
        compiler_params=pltpu.CompilerParams(vmem_limit_bytes=50 * MIB),
        name="gradient",
    )(rows, where, burn, state)


def divide(values, by):
    quotient = jnp.floor((values.astype(jnp.float32) + 0.5) * (1.0 / by)).astype(jnp.int32)
    return quotient, values - quotient * by


def locate(block_ids, per_x, per_y, blocks_y, gy_count):
    block_row, block_col = divide(block_ids, blocks_y)
    device_x, local_x = divide(block_row, per_x)
    device_y, local_y = divide(block_col, per_y)
    return device_x * gy_count + device_y, local_x * per_y + local_y


def on_device(
    adjoint_forcing,
    courant_x,
    courant_y,
    vertical_mix,
    tile_block,
    injection_level,
    plume_profile,
    burn_weight,
):
    levels, width_x, width_y = adjoint_forcing.shape
    gx_count = lax.axis_size("gx")
    gy_count = lax.axis_size("gy")
    total = gx_count * gy_count
    tiles_dev = injection_level.shape[0]
    capacity = 4
    per_x = width_x // TB
    per_y = width_y // TB
    blocks_y = per_y * gy_count
    me = lax.axis_index(("gx", "gy"))
    slot_table = tile_block.reshape(total, tiles_dev)
    source, local_block = locate(slot_table, per_x, per_y, blocks_y, gy_count)
    is_mine = (source == me).astype(jnp.int32)
    upto = jnp.triu(jnp.ones((tiles_dev, tiles_dev), jnp.bfloat16))
    rank = jnp.dot(
        is_mine.astype(jnp.bfloat16), upto, preferred_element_type=jnp.float32
    ).astype(jnp.int32) - 1
    slots = jnp.arange(capacity, dtype=jnp.int32)
    hits = (is_mine[:, None, :] == 1) & (rank[:, None, :] == slots[None, :, None])
    local = jnp.sum(jnp.where(hits, local_block[:, None, :], 0), axis=2)
    block_row, lane_at = divide(local, per_y)
    lane_at = lane_at * TB
    place = jnp.sum(jnp.where(hits, jnp.arange(tiles_dev, dtype=jnp.int32), 0), axis=2)
    share = min(tiles_dev, 128)
    table = jnp.concatenate(
        [
            (block_row * (width_y // 128) + lane_at // 128).T,
            (lane_at % 128 // TB).T,
            (place // share).T,
            (place % share).T,
        ],
        axis=0,
    )

    state_field, rows = stencil(
        adjoint_forcing, courant_x, courant_y, vertical_mix,
        injection_level.reshape(-1, share), table, plume_profile,
        gx_count, gy_count,
    )
    rows = rows.reshape(-1, 8, 128)

    own = lax.dynamic_slice_in_dim(source, me, 1, 0).reshape(tiles_dev)
    positions = jnp.arange(tiles_dev, dtype=jnp.int32)
    earlier = (own[None, :] == own[:, None]) & (positions[None, :] <= positions[:, None])
    arrival = jnp.sum(earlier.astype(jnp.int32), axis=1) - 1
    far, near = own // gy_count, own % gy_count
    spot = near % 4 * 4 + arrival
    row = (far * max(1, gy_count // 4) + near // 4) * 8 + spot % 8
    where = jnp.stack([row, spot // 8], axis=1)
    gradient_out, state_out = gradient(rows, where, burn_weight, state_field)
    return (state_out, gradient_out)


def solution(mesh):
    return jax.shard_map(
        on_device,
        mesh=mesh,
        in_specs=(
            P(None, "gx", "gy"),
            P(None, "gx", "gy"),
            P(None, "gx", "gy"),
            P(None, "gx", "gy"),
            P(),
            P(("gx", "gy")),
            P(),
            P(("gx", "gy"), None),
        ),
        out_specs=(P(None, "gx", "gy"), P(("gx", "gy"), None)),
        check_vma=False,
    )
```

```python
import functools

import jax
import jax.numpy as jnp
from jax import lax
from jax.experimental import pallas as pl
from jax.experimental.pallas import tpu as pltpu
from jax.sharding import PartitionSpec as P

ITERS = 4
TB = 8
SUB = 100
MESH = pl.DeviceIdType.MESH
MIB = 1024 * 1024


def fori(low, high, body):
    def step(i, carry):
        body(i)
        return carry

    lax.fori_loop(low, high, step, 0)


def stencil_kernel(
    f_hbm, cu_hbm, cv_hbm, k_hbm, own, table, profile, out, arrived,
    field, cu, cv, mix, work0, work1, ysend, yrecv, held, shared, level_of, weights,
    blocks, sums, depart, transit, again,
    load_sem, save_sem, xs_sem, xr_sem, ys_sem, yr_sem,
    send1, recv1, send2, recv2, send3, recv3, send4, recv4, level_sem,
):
    levels, rows, cols = field.shape
    tiles = cols // 128
    groups = rows // 16
    chunks = groups // 4
    work = (work0, work1)
    gx, gy = lax.axis_index("gx"), lax.axis_index("gy")
    nx, ny = lax.axis_size("gx"), lax.axis_size("gy")
    have_x = (gx > 0, gx < nx - 1)
    have_y = (gy > 0, gy < ny - 1)
    peer_x = ((jnp.maximum(gx - 1, 0), gy), (jnp.minimum(gx + 1, nx - 1), gy))
    peer_y = ((gx, jnp.maximum(gy - 1, 0)), (gx, jnp.minimum(gy + 1, ny - 1)))
    lane = lax.broadcasted_iota(jnp.int32, (16, 128), 1)
    odd = lane % 2 == 1

    pieces = [(0, 48, 0), (rows - 16, 16, 0)]
    pieces += [(64 * c - 16, 64, c) for c in range(1, chunks)]
    bounds = list(range(chunks + 1))

    def parts_copy(src, dst, sem):
        return [
            pltpu.make_async_copy(
                src.at[:, pl.ds(at, size), :], dst.at[:, pl.ds(at, size), :], sem.at[p]
            )
            for p, (at, size, _) in enumerate(pieces)
        ]

    load_f = parts_copy(f_hbm, field, load_sem.at[0])
    load_k = parts_copy(k_hbm, mix, load_sem.at[1])
    saves = parts_copy(field, out, save_sem)
    late = [
        pltpu.make_async_copy(cu_hbm, cu, load_sem.at[2, 0]),
        pltpu.make_async_copy(cv_hbm, cv, load_sem.at[2, 1]),
    ]
    for p in range(len(pieces)):
        load_f[p].start()
        load_k[p].start()
    for copy in late:
        copy.start()

    zero_row = jnp.zeros((1, 128), jnp.float32)

    def clear(l):
        for b in range(2):
            for j in range(tiles):
                work[b][l, j, 7:8, :] = zero_row
                work[b][l, j, rows + 8 : rows + 9, :] = zero_row

    fori(0, levels, clear)
    yrecv[...] = jnp.zeros_like(yrecv)

    barrier = pltpu.get_barrier_semaphore()

    def greet_y(o):
        pl.semaphore_signal(
            barrier, inc=1, device_id=(gx, lax.rem(gy + o, ny)), device_id_type=MESH
        )

    def greet_x(o):
        pl.semaphore_signal(
            barrier, inc=1, device_id=(lax.rem(gx + o, nx), gy), device_id_type=MESH
        )

    fori(1, ny, greet_y)
    fori(1, nx, greet_x)

    def share_y(o):
        return pltpu.make_async_remote_copy(
            src_ref=own,
            dst_ref=held.at[gy],
            send_sem=send1.at[o],
            recv_sem=recv1.at[o],
            device_id=(gx, lax.rem(gy + o, ny)),
            device_id_type=MESH,
        )

    def share_x(o):
        return pltpu.make_async_remote_copy(
            src_ref=held,
            dst_ref=shared.at[gx],
            send_sem=send2.at[o],
            recv_sem=recv2.at[o],
            device_id=(lax.rem(gx + o, nx), gy),
            device_id_type=MESH,
        )

    held[gy] = own[...]

    def enter():
        pl.semaphore_wait(barrier, nx + ny - 2)
        fori(1, ny, lambda o: share_y(o).start())

    def x_copy(n, side):
        b = n % 2
        src, dst = ((8, rows + 8), (rows + 7, 7))[side]
        return pltpu.make_async_remote_copy(
            src_ref=work[b].at[:, :, pl.ds(src, 1), :],
            dst_ref=work[b].at[:, :, pl.ds(dst, 1), :],
            send_sem=xs_sem.at[n, side],
            recv_sem=xr_sem.at[n, side],
            device_id=peer_x[side],
            device_id_type=MESH,
        )

    def y_copy(n, side, chunk):
        return pltpu.make_async_remote_copy(
            src_ref=ysend.at[n, chunk],
            dst_ref=yrecv.at[n, side, chunk],
            send_sem=ys_sem.at[n, side, chunk],
            recv_sem=yr_sem.at[n, side, chunk],
            device_id=peer_y[side],
            device_id_type=MESH,
        )

    def send_x(n):
        for side in range(2):
            @pl.when(have_x[side])
            def _():
                x_copy(n, side).start()

    def send_y(n, chunk):
        for side in range(2):
            @pl.when(have_y[side])
            def _():
                y_copy(n, side, chunk).start()

    def await_x(n):
        for side in range(2):
            @pl.when(have_x[side])
            def _():
                x_copy(n, 1 - side).wait_recv()

    def await_y(n, chunk):
        for side in range(2):
            @pl.when(have_y[side])
            def _():
                y_copy(n, 1 - side, chunk).wait_recv()

    def await_x_sent(n):
        for side in range(2):
            @pl.when(have_x[side])
            def _():
                x_copy(n, side).wait_send()

    def mixed(values, at, j):
        result, before = [], None
        for l in range(levels):
            total = values[l]
            if l < levels - 1:
                k = mix[l, pl.ds(at, 16), 128 * j : 128 * j + 128].astype(jnp.float32)
                flux = k * (values[l + 1] - values[l])
                total = total + flux
            if before is not None:
                total = total - before
            before = flux
            result.append(total)
        return result

    def pack(first, last, m):
        packed = None
        for l in range(levels):
            ends = jnp.where(lane == 0, first[l], last[l])
            if l:
                moved = pltpu.roll(ends, 2 * l, 1)
                packed = jnp.where((lane == 2 * l) | (lane == 2 * l - 1), moved, packed)
            else:
                packed = ends
        return packed if m == 0 else pltpu.roll(packed, 32 * m, 1)

    def moved_by_wind(b, at, here, j, halo):
        values = []
        for l in range(levels):
            c = work[b][l, j, pl.ds(here, 16), :]
            up = work[b][l, j, pl.ds(here + 1, 16), :]
            down = work[b][l, j, pl.ds(here - 1, 16), :]
            left = halo[l] if j == 0 else work[b][l, j - 1, pl.ds(here, 16), :]
            right = halo[l] if j == tiles - 1 else work[b][l, j + 1, pl.ds(here, 16), :]
            left = pltpu.roll(jnp.where(lane == 127, left, c), 1, 1)
            right = pltpu.roll(jnp.where(lane == 0, right, c), 127, 1)
            su = cu[l, pl.ds(at, 16), 128 * j : 128 * j + 128].astype(jnp.float32)
            sv = cv[l, pl.ds(at, 16), 128 * j : 128 * j + 128].astype(jnp.float32)
            total = c + jnp.abs(su) * (jnp.where(su > 0, up, down) - c)
            total = total + jnp.abs(sv) * (jnp.where(sv > 0, right, left) - c)
            values.append(total)
        return values

    def run(n, mode):
        source, target = (n + 1) % 2, n % 2

        def chunk_of(chunk):
            if mode != "first":
                await_y(n - 1, chunk)
            packed = []
            for m in range(4):
                i = jnp.where(chunk == 0, (0, groups - 1, 1, 2)[m], 4 * chunk - 1 + m)
                at = pl.multiple_of(16 * i, 16)
                here = pl.multiple_of(8 + 16 * i, 8)
                if mode != "first":
                    halo = jnp.where(odd, yrecv[n - 1, 1, chunk], yrecv[n - 1, 0, chunk])
                    halo = [
                        pltpu.roll(halo, (-32 * m - 2 * l) % 128, 1) if m or l else halo
                        for l in range(levels)
                    ]
                kept = []
                for j in range(tiles):
                    if mode == "first":
                        values = [
                            field[l, pl.ds(at, 16), 128 * j : 128 * j + 128]
                            for l in range(levels)
                        ]
                    else:
                        values = moved_by_wind(source, at, here, j, halo)
                    if mode == "last":
                        for l in range(levels):
                            field[l, pl.ds(at, 16), 128 * j : 128 * j + 128] = values[l]
                            for h in range(2):
                                block = (2 * i + h) * tiles + j
                                blocks[block, l] = values[l][8 * h : 8 * h + 8]
                    else:
                        result = mixed(values, at, j)
                        for l in range(levels):
                            work[target][l, j, pl.ds(here, 16), :] = result[l]
                if mode != "last":
                    ends = [
                        [work[target][l, j, pl.ds(here, 16), :] for l in range(levels)]
                        for j in (0, tiles - 1)
                    ]
                    packed.append(pack(ends[0], ends[1], m))
            if mode == "first":
                @pl.when(chunk == 0)
                def _():
                    enter()
            if mode != "last":
                ends = packed[0]
                for m in range(1, 4):
                    ends = jnp.where((lane >= 32 * m - 1) & (lane < 32 * m + 31), packed[m], ends)
                ysend[n, chunk] = ends
                send_y(n, chunk)

        def edges_first(chunk):
            @pl.when(chunk == 0)
            def _():
                if mode != "first":
                    await_x(n - 1)
                if mode == "middle" and n >= 2:
                    await_x_sent(n - 2)

            chunk_of(chunk)
            if mode != "last":
                @pl.when(chunk == 0)
                def _():
                    send_x(n)

        if mode == "middle":
            fori(0, chunks, edges_first)
        else:
            for low, high in zip(bounds, bounds[1:]):
                ready = [p for p, piece in enumerate(pieces) if piece[2] == low]
                if mode == "first":
                    for p in ready:
                        load_f[p].wait()
                        load_k[p].wait()
                fori(low, high, edges_first)
                if mode == "last":
                    for p in ready:
                        saves[p].start()

    run(0, "first")
    fori(1, ny, lambda o: share_y(o).wait_recv())
    fori(1, nx, lambda o: share_x(o).start())
    shared[gx] = held[...]
    for copy in late:
        copy.wait()
    for n in range(1, ITERS):
        run(n, "middle")
    fori(1, nx, lambda o: share_x(o).wait_recv())
    to_scalars = pltpu.make_async_copy(shared, level_of, level_sem)
    to_scalars.start()
    run(ITERS, "last")

    def spread(r):
        for l in range(levels):
            weights[r, l] = jnp.full((8, 128), profile[r, l], jnp.float32)

    fori(0, profile.shape[0], spread)
    to_scalars.wait()

    lane8 = lax.broadcasted_iota(jnp.int32, (8, 128), 1)

    def weigh(p, quad):
        for k in range(16):
            g = 4 * quad + k // 4
            block, lanes, high, low = (table[4 * a + k % 4, g * ny + p] for a in range(4))
            r = level_of[g, p, high, low]
            terms = [weights[r, l] * blocks[block, l] for l in range(levels)]
            while len(terms) > 1:
                terms = [a + b for a, b in zip(terms[::2], terms[1::2])]
            sums[quad, k] = jnp.where(lane8 // 8 == lanes, terms[0], 0.0)

    def settle(p):
        lists = [[sums[quad, k] for k in range(16)] for quad in range(nx // 4)]
        for bit in (8, 4, 2, 1):
            low = (lane8 // 8 & bit) == 0
            for quad, found in enumerate(lists):
                folded = []
                for a, b in zip(found[: len(found) // 2], found[len(found) // 2 :]):
                    keep, swap = jnp.where(low, a, b), jnp.where(low, b, a)
                    moved = pltpu.roll(swap, 8 * bit, 1)
                    if bit < 8:
                        moved = jnp.where(low, pltpu.roll(swap, 128 - 8 * bit, 1), moved)
                    folded.append(keep + moved)
                lists[quad] = folded
        for quad, found in enumerate(lists):
            depart[p, quad] = found[0]

    def along_y(o):
        to = lax.rem(gy + o, ny)
        return pltpu.make_async_remote_copy(
            src_ref=depart.at[to],
            dst_ref=transit.at[gy],
            send_sem=send3.at[o],
            recv_sem=recv3.at[o],
            device_id=(gx, to),
            device_id_type=MESH,
        )

    def along_x(o):
        to = lax.rem(gx + o, nx)
        return pltpu.make_async_remote_copy(
            src_ref=again.at[to],
            dst_ref=arrived.at[gx],
            send_sem=send4.at[o],
            recv_sem=recv4.at[o],
            device_id=(to, gy),
            device_id_type=MESH,
        )

    def depart_to(o):
        p = lax.rem(gy + o, ny)
        for quad in range(nx // 4):
            weigh(p, quad)
        settle(p)

        @pl.when(o < ny)
        def _():
            along_y(o).start()

    fori(1, ny + 1, depart_to)
    transit[gy] = depart[gy]
    fori(1, ny, lambda o: along_y(o).wait_recv())

    def pass_on(quad):
        for u in range(4):
            for h in range(again.shape[1]):
                packed = None
                for j in range(min(ny, 4)):
                    moved = transit[4 * h + j, quad]
                    if j != u:
                        moved = pltpu.roll(moved, 32 * (j - u) % 128, 1)
                    packed = moved if j == 0 else jnp.where(lane8 // 32 == j, moved, packed)
                again[4 * quad + u, h] = packed
            o = lax.rem(4 * quad + u + nx - gx, nx)

            @pl.when(o > 0)
            def _():
                along_x(o).start()

    quads = nx // 4
    fori(0, quads, lambda quad: pass_on(lax.rem(quad + gx // 4, quads)))
    arrived[gx] = again[gx]

    for n in (ITERS - 2, ITERS - 1):
        await_x_sent(n)

    def all_sent(n):
        for side in range(2):
            @pl.when(have_y[side])
            def _():
                for chunk in range(chunks):
                    y_copy(n, side, chunk).wait_send()

    for n in range(ITERS):
        all_sent(n)
    fori(1, ny, lambda o: share_y(o).wait_send())
    fori(1, nx, lambda o: share_x(o).wait_send())
    fori(1, ny, lambda o: along_y(o).wait_send())
    for save in saves:
        save.wait()
    fori(1, nx, lambda o: along_x(o).wait_recv())
    fori(1, nx, lambda o: along_x(o).wait_send())


def stencil(f, cu, cv, k, own, table, profile, nx, ny):
    levels, rows, cols = f.shape
    any_space = pl.BlockSpec(memory_space=pl.ANY)
    vmem = pl.BlockSpec(memory_space=pltpu.VMEM)
    tiles = cols // 128
    chunks = rows // 64
    smem = pl.BlockSpec(memory_space=pltpu.SMEM)
    halves = max(1, ny // 4)
    return pl.pallas_call(
        stencil_kernel,
        out_shape=(
            jax.ShapeDtypeStruct(f.shape, jnp.float32),
            jax.ShapeDtypeStruct((nx, halves, 8, 128), jnp.float32),
        ),
        in_specs=[any_space] * 4 + [vmem, smem, smem],
        out_specs=(any_space, vmem),
        scratch_shapes=[
            pltpu.VMEM(f.shape, jnp.float32),
            pltpu.VMEM(f.shape, jnp.bfloat16),
            pltpu.VMEM(f.shape, jnp.bfloat16),
            pltpu.VMEM(f.shape, jnp.bfloat16),
            pltpu.VMEM((levels, tiles, rows + 16, 128), jnp.float32),
            pltpu.VMEM((levels, tiles, rows + 16, 128), jnp.float32),
            pltpu.VMEM((ITERS, chunks, 16, 128), jnp.float32),
            pltpu.VMEM((ITERS, 2, chunks, 16, 128), jnp.float32),
            pltpu.VMEM((ny, *own.shape), jnp.int32),
            pltpu.VMEM((nx, ny, *own.shape), jnp.int32),
            pltpu.SMEM((nx, ny, *own.shape), jnp.int32),
            pltpu.VMEM((*profile.shape, 8, 128), jnp.float32),
            pltpu.VMEM((rows // 8 * tiles, levels, 8, 128), jnp.float32),
            pltpu.VMEM((nx // 4, 16, 8, 128), jnp.float32),
            pltpu.VMEM((ny, nx // 4, 8, 128), jnp.float32),
            pltpu.VMEM((ny, nx // 4, 8, 128), jnp.float32),
            pltpu.VMEM((nx, halves, 8, 128), jnp.float32),
            pltpu.SemaphoreType.DMA((3, 4)),
            pltpu.SemaphoreType.DMA((4,)),
            pltpu.SemaphoreType.DMA((ITERS, 2)),
            pltpu.SemaphoreType.DMA((ITERS, 2)),
            pltpu.SemaphoreType.DMA((ITERS, 2, chunks)),
            pltpu.SemaphoreType.DMA((ITERS, 2, chunks)),
            pltpu.SemaphoreType.DMA((ny,)),
            pltpu.SemaphoreType.DMA((ny,)),
            pltpu.SemaphoreType.DMA((nx,)),
            pltpu.SemaphoreType.DMA((nx,)),
            pltpu.SemaphoreType.DMA((ny,)),
            pltpu.SemaphoreType.DMA((ny,)),
            pltpu.SemaphoreType.DMA((nx,)),
            pltpu.SemaphoreType.DMA((nx,)),
            pltpu.SemaphoreType.DMA,
        ],
        compiler_params=pltpu.CompilerParams(
            collective_id=0, has_side_effects=True, vmem_limit_bytes=58 * MIB
        ),
        name="stencil",
    )(f, cu, cv, k, own, table, profile)


def gradient_kernel(rows, where, burn, state, out, state_out, column, held, copy_sem):
    step = pl.program_id(0)
    part = state.shape[0] // 4
    loads, saves = [], []
    for i in range(4):
        at = pl.ds(part * i, part)
        loads.append(pltpu.make_async_copy(state.at[at], held.at[at], copy_sem.at[0, i]))
        saves.append(pltpu.make_async_copy(held.at[at], state_out.at[at], copy_sem.at[1, i]))
    tiles_dev, width = burn.shape

    @pl.when(step == 0)
    def _():
        for load in loads:
            load.start()
        values = rows[...]
        sub = lax.broadcasted_iota(jnp.int32, values.shape, 1)
        group = lax.broadcasted_iota(jnp.int32, values.shape, 2) // 8
        for bit in (1, 2, 4):
            low = pltpu.roll(pltpu.roll(values, 8 - bit, 1), 8 * bit, 2)
            high = pltpu.roll(pltpu.roll(values, bit, 1), 128 - 8 * bit, 2)
            in_row, in_group = sub // bit % 2, group // bit % 2
            values = jnp.where(
                in_row == in_group, values, jnp.where(in_group == 1, low, high)
            )
        values = values.reshape(-1, 128)
        high = values.astype(jnp.bfloat16)
        rest = values - high.astype(jnp.float32)
        mid = rest.astype(jnp.bfloat16)
        low = (rest - mid.astype(jnp.float32)).astype(jnp.bfloat16)
        index = where[:, 0:1]
        half = where[:, 1:2]
        count = values.shape[0]
        onehot = (lax.broadcasted_iota(jnp.int32, (tiles_dev, count), 1) == index).astype(
            jnp.float32
        ).astype(jnp.bfloat16)
        lane = lax.broadcasted_iota(jnp.int32, (tiles_dev, 128), 1)
        parts = []
        for part in (high, mid, low):
            picked = jnp.dot(onehot, part, preferred_element_type=jnp.float32)
            parts.append(jnp.where(half == 1, pltpu.roll(picked, 64, 1), picked))
        column[:, 0:128] = jnp.where(lane < 64, parts[0], pltpu.roll(parts[1], 64, 1)).astype(
            jnp.bfloat16
        )
        column[:, 128:256] = jnp.where(lane < 64, parts[2], 0.0).astype(jnp.bfloat16)

    for i in range(4):
        @pl.when(step == i)
        def _():
            loads[i].wait()
            saves[i].start()

    cell = step * width + lax.broadcasted_iota(jnp.int32, (64, width), 1)
    start = SUB * lax.broadcasted_iota(jnp.int32, (64, width), 0)
    spread = ((cell >= start) & (cell < start + SUB)).astype(jnp.float32).astype(jnp.bfloat16)
    spread = jnp.concatenate([spread] * 4, axis=0)
    expanded = jnp.dot(column[...], spread, preferred_element_type=jnp.float32)
    out[...] = (burn[...].astype(jnp.float32) * expanded).astype(jnp.bfloat16)

    @pl.when(step == pl.num_programs(0) - 1)
    def _():
        for save in saves:
            save.wait()


def gradient(rows, where, burn, state):
    tiles_dev, fire = burn.shape
    width = 1280
    return pl.pallas_call(
        gradient_kernel,
        grid=(fire // width,),
        out_shape=(
            jax.ShapeDtypeStruct(burn.shape, jnp.bfloat16),
            jax.ShapeDtypeStruct(state.shape, state.dtype),
        ),
        in_specs=[
            pl.BlockSpec(rows.shape, lambda s: (0, 0, 0)),
            pl.BlockSpec(where.shape, lambda s: (0, 0)),
            pl.BlockSpec((tiles_dev, width), lambda s: (0, s)),
            pl.BlockSpec(memory_space=pl.ANY),
        ],
        out_specs=(
            pl.BlockSpec((tiles_dev, width), lambda s: (0, s)),
            pl.BlockSpec(memory_space=pl.ANY),
        ),
        scratch_shapes=[
            pltpu.VMEM((tiles_dev, 256), jnp.bfloat16),
            pltpu.VMEM(state.shape, state.dtype),
            pltpu.SemaphoreType.DMA((2, 4)),
        ],
        compiler_params=pltpu.CompilerParams(vmem_limit_bytes=50 * MIB),
        name="gradient",
    )(rows, where, burn, state)


def divide(values, by):
    quotient = jnp.floor((values.astype(jnp.float32) + 0.5) * (1.0 / by)).astype(jnp.int32)
    return quotient, values - quotient * by


def locate(block_ids, per_x, per_y, blocks_y, gy_count):
    block_row, block_col = divide(block_ids, blocks_y)
    device_x, local_x = divide(block_row, per_x)
    device_y, local_y = divide(block_col, per_y)
    return device_x * gy_count + device_y, local_x * per_y + local_y


def on_device(
    adjoint_forcing,
    courant_x,
    courant_y,
    vertical_mix,
    tile_block,
    injection_level,
    plume_profile,
    burn_weight,
):
    levels, width_x, width_y = adjoint_forcing.shape
    gx_count = lax.axis_size("gx")
    gy_count = lax.axis_size("gy")
    total = gx_count * gy_count
    tiles_dev = injection_level.shape[0]
    capacity = 4
    per_x = width_x // TB
    per_y = width_y // TB
    blocks_y = per_y * gy_count
    me = lax.axis_index(("gx", "gy"))
    slot_table = tile_block.reshape(total, tiles_dev)
    source, local_block = locate(slot_table, per_x, per_y, blocks_y, gy_count)
    is_mine = (source == me).astype(jnp.int32)
    upto = jnp.triu(jnp.ones((tiles_dev, tiles_dev), jnp.bfloat16))
    rank = jnp.dot(
        is_mine.astype(jnp.bfloat16), upto, preferred_element_type=jnp.float32
    ).astype(jnp.int32) - 1
    slots = jnp.arange(capacity, dtype=jnp.int32)
    hits = (is_mine[:, None, :] == 1) & (rank[:, None, :] == slots[None, :, None])
    local = jnp.sum(jnp.where(hits, local_block[:, None, :], 0), axis=2)
    block_row, lane_at = divide(local, per_y)
    lane_at = lane_at * TB
    place = jnp.sum(jnp.where(hits, jnp.arange(tiles_dev, dtype=jnp.int32), 0), axis=2)
    share = min(tiles_dev, 128)
    table = jnp.concatenate(
        [
            (block_row * (width_y // 128) + lane_at // 128).T,
            (lane_at % 128 // TB).T,
            (place // share).T,
            (place % share).T,
        ],
        axis=0,
    )

    state_field, rows = stencil(
        adjoint_forcing, courant_x, courant_y, vertical_mix,
        injection_level.reshape(-1, share), table, plume_profile,
        gx_count, gy_count,
    )
    rows = rows.reshape(-1, 8, 128)

    own = lax.dynamic_slice_in_dim(source, me, 1, 0).reshape(tiles_dev)
    positions = jnp.arange(tiles_dev, dtype=jnp.int32)
    earlier = (own[None, :] == own[:, None]) & (positions[None, :] <= positions[:, None])
    arrival = jnp.sum(earlier.astype(jnp.int32), axis=1) - 1
    far, near = own // gy_count, own % gy_count
    spot = near % 4 * 4 + arrival
    row = (far * max(1, gy_count // 4) + near // 4) * 8 + spot % 8
    where = jnp.stack([row, spot // 8], axis=1)
    gradient_out, state_out = gradient(rows, where, burn_weight, state_field)
    return (state_out, gradient_out)


def solution(mesh):
    return jax.shard_map(
        on_device,
        mesh=mesh,
        in_specs=(
            P(None, "gx", "gy"),
            P(None, "gx", "gy"),
            P(None, "gx", "gy"),
            P(None, "gx", "gy"),
            P(),
            P(("gx", "gy")),
            P(),
            P(("gx", "gy"), None),
        ),
        out_specs=(P(None, "gx", "gy"), P(("gx", "gy"), None)),
        check_vma=False,
    )
```
